256 devices in a mesh: dp: 16 (over y_hi, z), tensor: 16 (over x, y_lo, core).
Axes of the slice: x: 4, y: 4 (y_hi: 2, y_lo: 2; y = y_hi * 2 + y_lo), z: 8, core: 2. Of those that a mesh axis runs over, the one named last changes fastest.
Arguments:
- grad_out: bfloat16 [12288, 5120], P(('dp', 'tensor')), may hold values from -24 to 24
- gate_pre: bfloat16 [12288, 13824], P('dp', 'tensor'), may hold values from -8 to 8
- up_pre: bfloat16 [12288, 13824], P('dp', 'tensor'), may hold values from -6 to 6
- down_weight: bfloat16 [5120, 13824], P('dp', 'tensor'), may hold values from -0.078125 to 0.078125
Outputs:
- grad_gate: bfloat16 [12288, 13824], P('dp', 'tensor')
- grad_up: bfloat16 [12288, 13824], P('dp', 'tensor')
- grad_down: bfloat16 [5120, 13824], P('dp', 'tensor')
The draws below stay inside these ranges and needn't reach their ends.
All inputs are finite; a program needn't handle non-finite values.
Results may differ from the reference program's by a relative error of at most 0.019.
Values may be sent and summed in bfloat16 or wider, within the bound.
No kernel may reach another device: no remote copies, remote signals or barrier semaphores. Data moves between devices by JAX's collectives and lax.ppermute only.
A program may use at most 128 MiB of HBM per device.

```python
import jax
import jax.numpy as jnp
from jax import lax

D = 5120
HIDDEN_SIZE = 13824
GROUP_TOK = 768
TOKENS = 12288
N_DP = 16


def raised(values, rng, source, target, shards_of, factor):
    def block_of(dim):
        return (jnp.arange(values.shape[dim]) // (values.shape[dim] // shards_of)).reshape((-1,) + (1,) * (values.ndim - 1 - dim))

    one_side = jax.random.permutation(rng, shards_of)[block_of(target)]
    other_side = (block_of(target) + shards_of // 2) % shards_of
    return jnp.where((block_of(source) == one_side) | (block_of(source) == other_side), factor * values, values)


def block_levels(key, dims, cuts, least, top_value):
    def one(position, parts):
        draws = jax.random.uniform(jax.random.fold_in(jax.random.fold_in(key, 6), position), (parts,), jnp.float32, least / len(cuts), top_value / len(cuts))
        return jnp.repeat(jnp.exp(draws), dims[position] // parts).reshape((-1,) + (1,) * (len(dims) - position - 1))

    loudness = one(*cuts[0])
    for cut in cuts[1:]:
        loudness = loudness * one(*cut)
    return loudness


def scatter_about(own_key, dims, width, reach, shards=(), kind=jnp.bfloat16):
    entries = width * jax.random.normal(own_key, dims, jnp.float32)
    if shards:
        entries = entries * block_levels(own_key, dims, shards, -0.22, 0.18)
    return jnp.clip(entries, -reach, reach).astype(kind)


def heavy_noise(rng, dims, scale, reach, split, heavy, kind=jnp.bfloat16):
    array = scale * jax.random.normal(rng, dims, jnp.float32)
    if split:
        array = array * block_levels(rng, dims, split, -0.22, 0.18)
    return jnp.clip(raised(array, jax.random.fold_in(rng, 3), *heavy), -reach, reach).astype(kind)


def setup_inputs(seed: int = 0) -> dict:
    streams_of = jax.random.split(jax.random.key(seed), 5)
    return {
        "grad_out": heavy_noise(streams_of[0], (TOKENS, D), 1.0, 24.0, ((0, 256),), (0, 1, 256, 6.0)),
        "gate_pre": scatter_about(streams_of[1], (TOKENS, HIDDEN_SIZE), 2.0, 8.0, ((0, 16), (1, 16))),
        "up_pre": scatter_about(streams_of[2], (TOKENS, HIDDEN_SIZE), 1.0, 6.0, ((0, 16), (1, 16))),
        "down_weight": scatter_about(streams_of[3], (D, HIDDEN_SIZE), D ** -0.5, 0.078125, ((0, 16), (1, 16))),
    }


def reference(grad_out, gate_pre, up_pre, down_weight):
    grad_blocks = grad_out.reshape(N_DP, GROUP_TOK, D)
    gate_blocks = gate_pre.reshape(N_DP, GROUP_TOK, HIDDEN_SIZE)
    up_blocks = up_pre.reshape(N_DP, GROUP_TOK, HIDDEN_SIZE)

    def one_batch(running_sum, inputs):
        grad_rows, gate_rows, up_rows = inputs
        gate32 = gate_rows.astype(jnp.float32)
        up32 = up_rows.astype(jnp.float32)
        sigmoid_gate = jax.nn.sigmoid(gate32)
        gate_silu = gate32 * sigmoid_gate
        hidden = (gate_silu * up32).astype(jnp.bfloat16)
        grad_hidden = jnp.dot(grad_rows, down_weight, preferred_element_type=jnp.float32)
        grad_up = (grad_hidden * gate_silu).astype(jnp.bfloat16)
        grad_gate = (grad_hidden * up32 * sigmoid_gate * (1.0 + gate32 * (1.0 - sigmoid_gate))).astype(jnp.bfloat16)
        batch_term = jnp.dot(grad_rows.astype(jnp.float32).T, hidden.astype(jnp.float32), preferred_element_type=jnp.float32).astype(jnp.bfloat16)
        return running_sum + batch_term.astype(jnp.float32), (grad_gate, grad_up)

    zero_start = jnp.zeros((D, HIDDEN_SIZE), jnp.float32)
    total_grad, (grad_gate, grad_up) = lax.scan(one_batch, zero_start, (grad_blocks, gate_blocks, up_blocks))
    return grad_gate.reshape(TOKENS, HIDDEN_SIZE), grad_up.reshape(TOKENS, HIDDEN_SIZE), total_grad.astype(jnp.bfloat16)
```

```python
import functools

import jax
import jax.numpy as jnp
from jax import lax
from jax.experimental import pallas as pl
from jax.experimental.pallas import tpu as pltpu
from jax.sharding import Mesh, PartitionSpec as P

AXES = ("yh", "z", "x", "yl", "c")
SIZES = (2, 8, 4, 2, 2)
NZ = 8
NEAR, LATE = (4, 3, 5, 2), (6, 1, 7, 0)
ANYWHERE = pl.BlockSpec(memory_space=pl.ANY)


def permutation(move):
    pairs = []
    for src in range(256):
        rest, c = divmod(src, 2)
        rest, yl = divmod(rest, 2)
        rest, x = divmod(rest, 4)
        yh, z = divmod(rest, 8)
        y, z, x, c = move(2 * yh + yl, z, x, c)
        y, z, x = y % 4, z % 8, x % 4
        dst = ((((y // 2) * 8 + z) * 4 + x) * 2 + y % 2) * 2 + c
        pairs.append((src, dst))
    return pairs


def along_z(step):
    return permutation(lambda y, z, x, c: (y, z + step, x, c))


RING_Y = permutation(lambda y, z, x, c: (y + 1 - 2 * c, z, x, c))
RING_X = permutation(lambda y, z, x, c: (y, z, x + 1 - 2 * c, c))
PARTNER = permutation(lambda y, z, x, c: (y + 2, z, x, c))
CORES = permutation(lambda y, z, x, c: (y, z, x, 1 - c))


def send(value, pairs):
    return lax.ppermute(value, AXES, pairs)


def params(mib):
    return pltpu.CompilerParams(vmem_limit_bytes=mib * 2**20)


def columns_kernel(place, grad_ref, _, near_ref, late_ref):
    rows, depth = grad_ref.shape
    feats = depth // (2 * NZ)
    shift = lax.rem((NZ - place[0]) * feats, depth // 2)
    for side in range(2):
        part = grad_ref[:, side * depth // 2 : (side + 1) * depth // 2].astype(jnp.float32)
        part = pltpu.roll(part, shift, 1).astype(jnp.bfloat16)
        for ref, rels in ((near_ref, NEAR), (late_ref, LATE)):
            for i, rel in enumerate(rels):
                at = (2 * i + side) * feats
                ref[:, at : at + feats] = part[:, rel * feats : (rel + 1) * feats]


def columns(place, grad_out, after):
    rows, depth = grad_out.shape
    out = jax.ShapeDtypeStruct((rows, depth // 2), jnp.bfloat16)
    return pl.pallas_call(
        columns_kernel,
        grid_spec=pltpu.PrefetchScalarGridSpec(
            num_scalar_prefetch=1,
            grid=(1,),
            in_specs=[pl.BlockSpec((rows, depth), lambda k, place: (0, 0)), ANYWHERE],
            out_specs=[pl.BlockSpec((rows, depth // 2), lambda k, place: (0, 0))] * 2,
        ),
        out_shape=[out, out],
        compiler_params=params(8),
        cost_estimate=pl.CostEstimate(flops=10 * rows * depth, bytes_accessed=4 * rows * depth, transcendentals=0),
        name="columns",
    )(place, grad_out, after)


def slab(half):
    return half // 3 if half % 48 == 0 else half


def hidden_kernel(place, gate_keep, up_keep, gate_send, up_send, keep_ref, send_ref):
    for gate_ref, up_ref, out_ref in ((gate_keep, up_keep, keep_ref), (gate_send, up_send, send_ref)):
        gate = gate_ref[...].astype(jnp.float32)
        out_ref[...] = (gate * jax.nn.sigmoid(gate) * up_ref[...].astype(jnp.float32)).astype(jnp.bfloat16)


def hidden_halves(place, gate, up):
    width, tokens = gate.shape
    rows = slab(width // 2)
    steps = width // 2 // rows
    keep_in = pl.BlockSpec((rows, tokens), lambda k, place: (place[1] * steps + k, 0))
    send_in = pl.BlockSpec((rows, tokens), lambda k, place: ((1 - place[1]) * steps + k, 0))
    block_out = pl.BlockSpec((rows, tokens), lambda k, place: (k, 0))
    out = jax.ShapeDtypeStruct((width // 2, tokens), jnp.bfloat16)
    return pl.pallas_call(
        hidden_kernel,
        grid_spec=pltpu.PrefetchScalarGridSpec(
            num_scalar_prefetch=1,
            grid=(steps,),
            in_specs=[keep_in, keep_in, send_in, send_in],
            out_specs=[block_out, block_out],
        ),
        out_shape=[out, out],
        compiler_params=params(12),
        cost_estimate=pl.CostEstimate(
            flops=6 * tokens * width, bytes_accessed=6 * tokens * width, transcendentals=2 * tokens * width
        ),
        name="hidden_halves",
    )(place, gate, up, gate, up)


def fetch(place, pieces, at, slot, sem):
    (refs, starts), x_first = pieces
    rows = refs[0].shape[0] // 4
    wide = slot.shape[1]
    x, y, c = place[2], 2 * place[1] + place[3], place[4]
    for dc in range(2):
        core = c ^ dc
        way = 2 * core - 1
        for outer in range(4):
            for inner in range(4):
                dx, dy = (inner, outer) if x_first else (outer, inner)
                from_x, from_y = (x + way * dx) & 3, (y + way * dy) & 3
                block = ((from_y >> 1) ^ place[1]) * 16 + from_x * 4 + (from_y & 1) * 2 + core
                to = pl.ds(pl.multiple_of(block * rows, rows), rows)
                k = 4 * dc + outer
                pltpu.make_async_copy(
                    refs[k].at[pl.ds(starts[k] + inner * rows, rows), pl.ds(at, wide)], slot.at[to, :], sem
                ).start()


def arrived(slot, sem):
    pltpu.make_async_copy(slot, slot, sem).wait()


def terms_kernel(start, starts, x_first, cut, place, keep_ref, got_ref, *refs):
    pieces, outs, slots, sems = ((refs[:8], starts), x_first), refs[8:-2], refs[-2], refs[-1]
    step, steps = pl.program_id(0), pl.num_programs(0)
    wide = slots.shape[2]
    tokens = keep_ref.shape[1]

    def bring(i):
        at = pl.multiple_of((start + i) * wide, wide)
        fetch(place, pieces, at, slots.at[lax.rem(i, 2)], sems.at[lax.rem(i, 2)])

    @pl.when(step == 0)
    def _():
        bring(step)

    @pl.when(step + 1 < steps)
    def _():
        bring(step + 1)

    now = lax.rem(step, 2)
    arrived(slots.at[now], sems.at[now])
    term = jnp.dot(keep_ref[...], slots[now, :tokens], preferred_element_type=jnp.float32) + jnp.dot(
        got_ref[...], slots[now, tokens:], preferred_element_type=jnp.float32
    )
    if cut:
        outs[0][...] = term[:cut].astype(jnp.bfloat16)
        outs[1][...] = term[cut:].astype(jnp.bfloat16)
    else:
        outs[0][0] = term.astype(jnp.bfloat16)


def batch_terms(place, keep, got, pieces, wide, start, steps, cut=0):
    half, tokens = keep.shape
    (arrays, starts), x_first = pieces
    whole = pl.BlockSpec((half, tokens), lambda k, place: (0, 0))
    if cut:
        shapes = [(cut, wide), (half - cut, wide)]
        out_shape = [jax.ShapeDtypeStruct(shape, jnp.bfloat16) for shape in shapes]
        out_specs = [pl.BlockSpec(shape, lambda k, place: (0, 0)) for shape in shapes]
    else:
        out_shape = jax.ShapeDtypeStruct((steps, half, wide), jnp.bfloat16)
        out_specs = pl.BlockSpec((1, half, wide), lambda k, place: (k, 0, 0))

    return pl.pallas_call(
        functools.partial(terms_kernel, start, starts, x_first, cut),
        grid_spec=pltpu.PrefetchScalarGridSpec(
            num_scalar_prefetch=1,
            grid=(steps,),
            in_specs=[whole, whole] + [ANYWHERE] * len(arrays),
            out_specs=out_specs,
            scratch_shapes=[pltpu.VMEM((2, 2 * tokens, wide), jnp.bfloat16), pltpu.SemaphoreType.DMA((2,))],
        ),
        out_shape=out_shape,
        compiler_params=params(20),
        name="batch_terms",
    )(place, keep, got, *arrays)


def grad_hidden_kernel(starts, x_first, parts, last, place, *refs):
    n = sum(parts)
    pieces, weights, rest = ((refs[:8], starts), x_first), refs[8 : 8 + n], refs[8 + n :]
    if last:
        before_ref, mine_ref, other_ref, total, slots, held, sems, weight_sems = rest
    else:
        total, slots, held, sems, weight_sems = rest
    step, steps = pl.program_id(0), pl.num_programs(0)
    wide = slots.shape[2]
    chunk = wide // 2
    tokens = total.shape[0] // 2

    def bring(i):
        now = lax.rem(i, 2)
        fetch(place, pieces, pl.multiple_of(i * wide, wide), slots.at[now], sems.at[now])
        for k in range(len(parts)):

            @pl.when(i == k // 2)
            def _(k=k):
                to = 0
                for weight in weights[sum(parts[:k]) : sum(parts[: k + 1])]:
                    rows = weight.shape[0]
                    where = held.at[now, pl.ds(to, rows), pl.ds(k % 2 * chunk, chunk)]
                    pltpu.make_async_copy(weight, where, weight_sems.at[now]).start()
                    to += rows

    @pl.when(step == 0)
    def _():
        bring(step)

    @pl.when(step + 1 < steps)
    def _():
        bring(step + 1)

    now = lax.rem(step, 2)
    arrived(held.at[now], weight_sems.at[now])
    arrived(slots.at[now], sems.at[now])
    product = lax.dot_general(
        slots[now], held[now], (((1,), (1,)), ((), ())), preferred_element_type=jnp.float32
    )

    @pl.when(step == 0)
    def _():
        total[...] = product + before_ref[...] if last else product

    @pl.when(step > 0)
    def _():
        total[...] += product

    if last:

        @pl.when(step + 1 == steps)
        def _():
            mine_ref[...] = total[:tokens].T
            other_ref[...] = total[tokens:].T.astype(jnp.bfloat16)


def grad_hidden_part(place, pieces, weights, parts, before=None):
    half, wide = weights[-1].shape
    (arrays, starts), x_first = pieces
    tokens = 4 * arrays[0].shape[0]
    args = [*arrays, *weights]
    full = pl.BlockSpec((2 * tokens, half), lambda k, place: (0, 0))
    block = pl.BlockSpec((half, tokens), lambda k, place: (0, 0))
    in_specs = [ANYWHERE] * len(args)
    scratch = [
        pltpu.VMEM((2, 2 * tokens, 2 * wide), jnp.bfloat16),
        pltpu.VMEM((2, half, 2 * wide), jnp.bfloat16),
        pltpu.SemaphoreType.DMA((2,)),
        pltpu.SemaphoreType.DMA((2,)),
    ]
    last = before is not None
    if last:
        args.append(before)
        in_specs.append(full)
        out_specs = [block, block]
        out_shape = [
            jax.ShapeDtypeStruct((half, tokens), jnp.float32),
            jax.ShapeDtypeStruct((half, tokens), jnp.bfloat16),
        ]
        scratch = [pltpu.VMEM((2 * tokens, half), jnp.float32)] + scratch
    else:
        out_specs, out_shape = full, jax.ShapeDtypeStruct((2 * tokens, half), jnp.float32)
    return pl.pallas_call(
        functools.partial(grad_hidden_kernel, starts, x_first, parts, last),
        grid_spec=pltpu.PrefetchScalarGridSpec(
            num_scalar_prefetch=1, grid=(len(parts) // 2,), in_specs=in_specs, out_specs=out_specs, scratch_shapes=scratch
        ),
        out_shape=out_shape,
        compiler_params=params(32),
        name="grad_hidden",
    )(place, *args)


def gate_kernel(place, gate_ref, up_ref, grad_ref, *refs):
    grad_gate_ref, grad_up_ref = refs[-2:]
    gate = gate_ref[...].astype(jnp.float32)
    up = up_ref[...].astype(jnp.float32)
    grad_hidden = grad_ref[...].astype(jnp.float32)
    sigmoid = jax.nn.sigmoid(gate)
    grad_up_ref[...] = (grad_hidden * (gate * sigmoid)).astype(jnp.bfloat16)
    grad_gate_ref[...] = (grad_hidden * up * sigmoid * (1.0 + gate * (1.0 - sigmoid))).astype(jnp.bfloat16)


def gate_grads(place, gate, up, grad_hidden, before):
    width, tokens = gate.shape
    rows = slab(width // 2)
    steps = width // 2 // rows
    own = not before
    block = pl.BlockSpec((rows, tokens), lambda k, place: ((place[1] if own else 1 - place[1]) * steps + k, 0))
    block_half = pl.BlockSpec((rows, tokens), lambda k, place: (k, 0))
    out = jax.ShapeDtypeStruct((width, tokens), jnp.bfloat16)
    return pl.pallas_call(
        gate_kernel,
        grid_spec=pltpu.PrefetchScalarGridSpec(
            num_scalar_prefetch=1,
            grid=(steps,),
            in_specs=[block, block, block_half] + [ANYWHERE] * len(before),
            out_specs=[block, block],
        ),
        out_shape=[out, out],
        input_output_aliases={} if own else {4: 0, 5: 1},
        compiler_params=params(12),
        cost_estimate=pl.CostEstimate(
            flops=6 * tokens * width, bytes_accessed=6 * tokens * width, transcendentals=tokens * width
        ),
        name="gate_grads",
    )(place, gate, up, grad_hidden, *before)


def together(*arrays, extra=()):
    n = len(arrays)
    dtype, wide = jnp.bfloat16, [arrays[parts[0][0]].shape[1] for parts in extra]
    heights = [sum(part[2] for part in parts) for parts in extra]

    def body(*refs):
        ins, outs, sem = refs[:n], refs[2 * n : 2 * n + len(extra)], refs[-1]
        copies = []
        for parts, out in zip(extra, outs):
            to = 0
            for i, row, rows in parts:
                copies.append(
                    pltpu.make_async_copy(
                        ins[i].at[pl.ds(row, rows), :], out.at[pl.ds(to, rows), :], sem.at[len(copies)]
                    )
                )
                to += rows
        for copy in copies:
            copy.start()
        for copy in copies:
            copy.wait()

    whole = pl.BlockSpec(memory_space=pltpu.VMEM)
    count = sum(len(parts) for parts in extra)
    outs = pl.pallas_call(
        body,
        in_specs=[ANYWHERE] * n,
        out_specs=[ANYWHERE] * n + [whole] * len(extra),
        out_shape=[jax.ShapeDtypeStruct(array.shape, array.dtype) for array in arrays]
        + [jax.ShapeDtypeStruct(shape, dtype) for shape in zip(heights, wide)],
        input_output_aliases={i: i for i in range(n)},
        scratch_shapes=[pltpu.SemaphoreType.DMA((max(count, 1),))],
        compiler_params=params(4),
        name="together",
    )(*arrays)
    return outs


def lines(first, second):
    rows, wide = first[0].shape

    def body(*refs):
        for k, ref in enumerate(refs[:8]):
            part = ref[...]
            refs[8 + k // 4][k % 4 * rows : (k % 4 + 1) * rows, :] = part
            refs[10][k * rows : (k + 1) * rows, :] = part

    def block(n):
        return pl.BlockSpec((n * rows, wide), lambda: (0, 0))

    def shape(n):
        return jax.ShapeDtypeStruct((n * rows, wide), jnp.bfloat16)

    return pl.pallas_call(
        body,
        in_specs=[block(1)] * 8,
        out_specs=[block(4), block(4), block(8)],
        out_shape=[shape(4), shape(4), shape(8)],
        compiler_params=params(12),
        name="lines",
    )(*first, *second)


def pass_on(terms_up, i_up, terms_down, i_down, upward, downward):
    _, half, wide = terms_up.shape
    cut = upward.shape[0]
    whole = cut == half

    def body(up_ref, down_ref, upward_ref, downward_ref, rise_ref, fall_ref):
        def plus(a, b):
            return (a.astype(jnp.float32) + b.astype(jnp.float32)).astype(jnp.bfloat16)

        if whole:
            rise_ref[...] = plus(up_ref[0], upward_ref[...])
            fall_ref[...] = plus(down_ref[0], downward_ref[...])
        else:
            rise_ref[:cut] = plus(up_ref[0, :cut], upward_ref[...])
            rise_ref[cut:] = up_ref[0, cut:]
            fall_ref[:cut] = down_ref[0, :cut]
            fall_ref[cut:] = plus(down_ref[0, cut:], downward_ref[...])

    out = jax.ShapeDtypeStruct((half, wide), jnp.bfloat16)
    return pl.pallas_call(
        body,
        grid=(1,),
        in_specs=[
            pl.BlockSpec((1, half, wide), lambda k: (i_up, 0, 0)),
            pl.BlockSpec((1, half, wide), lambda k: (i_down, 0, 0)),
            pl.BlockSpec(upward.shape, lambda k: (0, 0)),
            pl.BlockSpec(downward.shape, lambda k: (0, 0)),
        ],
        out_specs=[pl.BlockSpec((half, wide), lambda k: (0, 0))] * 2,
        out_shape=[out, out],
        compiler_params=params(16),
        name="pass_on",
    )(terms_up, terms_down, upward, downward)


def last_sum(place, terms, i, upward, downward):
    _, half, wide = terms.shape
    feats = wide // 2

    def body(place, term_ref, upward_ref, downward_ref, keep_ref, send_ref):
        total = (
            term_ref[0].astype(jnp.float32)
            + upward_ref[...].astype(jnp.float32)
            + downward_ref[...].astype(jnp.float32)
        ).astype(jnp.bfloat16)
        first = place[1] == 0

        @pl.when(first)
        def _():
            keep_ref[...] = total[:, :feats]
            send_ref[...] = total[:, feats:]

        @pl.when(jnp.logical_not(first))
        def _():
            keep_ref[...] = total[:, feats:]
            send_ref[...] = total[:, :feats]

    out = jax.ShapeDtypeStruct((half, feats), jnp.bfloat16)
    full = pl.BlockSpec((half, wide), lambda k, place: (0, 0))
    return pl.pallas_call(
        body,
        grid_spec=pltpu.PrefetchScalarGridSpec(
            num_scalar_prefetch=1,
            grid=(1,),
            in_specs=[pl.BlockSpec((1, half, wide), lambda k, place: (i, 0, 0)), full, full],
            out_specs=[pl.BlockSpec((half, feats), lambda k, place: (0, 0))] * 2,
        ),
        out_shape=[out, out],
        compiler_params=params(16),
        name="last_sum",
    )(place, terms, upward, downward)


def local(grad_out, gate_pre, up_pre, down_weight):
    f32, bf16 = jnp.float32, jnp.bfloat16
    yh, z, x, yl, c = [lax.axis_index(name) for name in AXES]
    place = jnp.stack([z, yh, x, yl, c]).astype(jnp.int32)
    tokens, width = gate_pre.shape
    feats = down_weight.shape[0]
    half, wide = width // 2, 2 * feats
    cut = half // 32 * 16 + half % 32 // 16 * 16

    turned = down_weight.T
    kept = lax.dynamic_slice(turned, (yh * half, 0), (half, feats))
    leaving = lax.dynamic_slice(turned, ((1 - yh) * half, 0), (half, feats))
    near, late = columns(place, grad_out, leaving)
    kept_hidden, sent_hidden = hidden_halves(place, gate_pre.T, up_pre.T)

    got, near_1, late_1 = send(leaving, PARTNER), send(near, RING_Y), send(late, RING_X)
    got, near_1, late_1, sent_hidden = together(got, near_1, late_1, sent_hidden)
    pair = jnp.concatenate([jnp.where(yh == 0, kept, got), jnp.where(yh == 0, got, kept)], axis=1)
    up_1, down_1 = send(pair, along_z(1)), send(pair, along_z(-1))
    near_2, late_2 = send(near_1, RING_Y), send(late_1, RING_X)
    near_2, late_2, sent_hidden = together(near_2, late_2, sent_hidden)
    got_hidden = send(sent_hidden, PARTNER)
    near_3, late_3 = send(near_2, RING_Y), send(late_2, RING_X)
    near_0, late_0, both_0 = lines((near, near_1, near_2, near_3), (late, late_1, late_2, late_3))
    near_0, late_0, both_0, up_1, down_1 = together(near_0, late_0, both_0, up_1, down_1)

    rows = near_0.shape[0]
    joint = ((2, 0, rows), (3, 0, rows))
    up_2, down_2 = send(up_1, along_z(1)), send(down_1, along_z(-1))
    near_1, late_1 = send(near_0, RING_X), send(late_0, RING_Y)
    up_2, down_2, near_1, late_1, got_hidden, both_0, both_1 = together(
        up_2, down_2, near_1, late_1, got_hidden, both_0, extra=[joint]
    )

    up_3, down_3 = send(up_2, along_z(1)), send(down_2, along_z(-1))
    near_2, late_2 = send(near_1, RING_X), send(late_1, RING_Y)
    swap_0 = send(both_0, CORES)
    up_3, down_3, near_2, late_2, swap_0, both_1, far_up, far_down = together(
        up_3, down_3, near_2, late_2, swap_0, both_1, extra=[((0, 0, cut),), ((1, cut, half - cut),)]
    )

    far_up, far_down = send(far_up, along_z(1)), send(far_down, along_z(-1))
    near_3, late_3 = send(near_2, RING_X), send(late_2, RING_Y)
    swap_1 = send(both_1, CORES)
    far_up, far_down, near_3, late_3, swap_1 = together(far_up, far_down, near_3, late_3, swap_1)

    near_swapped = [swap_0, swap_1, send(near_2, CORES), send(near_3, CORES)]
    near = ([near_0, near_1, near_2, near_3, *near_swapped], (0,) * 8), False
    late_swapped = [swap_0, swap_1, send(late_2, CORES), send(late_3, CORES)]
    late = ([late_0, late_1, late_2, late_3, *late_swapped], (0,) * 4 + (rows, rows, 0, 0)), True

    make = functools.partial(batch_terms, place, kept_hidden, got_hidden)
    farthest = make(near, wide, 0, 1, cut)
    near_terms = make(near, wide, 1, 3)
    late_first = make(late, wide, 0, 1)
    late_terms = make(late, wide, 1, 3)
    subtotal = grad_hidden_part(place, near, [far_up, far_down, down_3, up_3, down_2], (2, 1, 1, 1))

    upward, downward = send(farthest[0], along_z(1)), send(farthest[1], along_z(-1))
    rise, fall = pass_on(near_terms, 0, near_terms, 1, upward, downward)
    upward, downward = send(rise, along_z(1)), send(fall, along_z(-1))
    upward, downward, subtotal = together(upward, downward, subtotal)
    mine, other = grad_hidden_part(place, late, [up_2, down_1, up_1, pair], (1, 1, 1, 1), subtotal)
    rise, fall = pass_on(near_terms, 2, late_first, 0, upward, downward)
    upward, downward = send(rise, along_z(1)), send(fall, along_z(-1))
    rise, fall = pass_on(late_terms, 0, late_terms, 1, upward, downward)
    upward, downward = send(rise, along_z(1)), send(fall, along_z(-1))
    kept, leaving = last_sum(place, late_terms, 2, upward, downward)
    got = send(leaving, PARTNER)
    grad_down = jnp.concatenate([jnp.where(yh == 0, kept, got), jnp.where(yh == 0, got, kept)], axis=0).T

    other = send(other, PARTNER)
    grads = gate_grads(place, gate_pre.T, up_pre.T, mine, ())
    grad_gate, grad_up = gate_grads(place, gate_pre.T, up_pre.T, other, tuple(grads))
    return grad_gate.T, grad_up.T, grad_down


def solution(mesh):
    inner = Mesh(mesh.devices.reshape(SIZES), AXES)
    dp, tensor = ("yh", "z"), ("x", "yl", "c")
    placed = (P(dp + tensor, None), P(dp, tensor), P(dp, tensor), P(dp, tensor))
    return jax.shard_map(
        local,
        mesh=inner,
        in_specs=placed,
        out_specs=(P(dp, tensor), P(dp, tensor), P(dp, tensor)),
        check_vma=False,
    )
```

```python
import functools

import jax
import jax.numpy as jnp
from jax import lax
from jax.experimental import pallas as pl
from jax.experimental.pallas import tpu as pltpu
from jax.sharding import Mesh, PartitionSpec as P

AXES = ("yh", "z", "x", "yl", "c")
SIZES = (2, 8, 4, 2, 2)
NZ = 8
NEAR, LATE = (4, 3, 5, 2), (6, 1, 7, 0)
ANYWHERE = pl.BlockSpec(memory_space=pl.ANY)


def permutation(move):
    pairs = []
    for src in range(256):
        rest, c = divmod(src, 2)
        rest, yl = divmod(rest, 2)
        rest, x = divmod(rest, 4)
        yh, z = divmod(rest, 8)
        y, z, x, c = move(2 * yh + yl, z, x, c)
        y, z, x = y % 4, z % 8, x % 4
        dst = ((((y // 2) * 8 + z) * 4 + x) * 2 + y % 2) * 2 + c
        pairs.append((src, dst))
    return pairs


def along_z(step):
    return permutation(lambda y, z, x, c: (y, z + step, x, c))


RING_Y = permutation(lambda y, z, x, c: (y + 1 - 2 * c, z, x, c))
RING_X = permutation(lambda y, z, x, c: (y, z, x + 1 - 2 * c, c))
BACK_Y = permutation(lambda y, z, x, c: (y - 1 + 2 * c, z, x, c))
BACK_X = permutation(lambda y, z, x, c: (y, z, x - 1 + 2 * c, c))
PARTNER = permutation(lambda y, z, x, c: (y + 2, z, x, c))
CORES = permutation(lambda y, z, x, c: (y, z, x, 1 - c))


def send(value, pairs):
    return lax.ppermute(value, AXES, pairs)


def params(mib):
    return pltpu.CompilerParams(vmem_limit_bytes=mib * 2**20)


def prepare_kernel(place, grad_ref, weight_ref, near_ref, late_ref, keep_ref, send_ref):
    rows, depth = grad_ref.shape
    feats = depth // (2 * NZ)
    half = keep_ref.shape[0]
    turned = weight_ref[...].astype(jnp.float32).T.astype(jnp.bfloat16)
    first = place[1] == 0

    @pl.when(first)
    def _():
        keep_ref[...] = turned[:half]
        send_ref[...] = turned[half:]

    @pl.when(jnp.logical_not(first))
    def _():
        keep_ref[...] = turned[half:]
        send_ref[...] = turned[:half]

    shift = lax.rem((NZ - place[0]) * feats, depth // 2)
    for side in range(2):
        part = grad_ref[:, side * depth // 2 : (side + 1) * depth // 2].astype(jnp.float32)
        part = pltpu.roll(part, shift, 1).astype(jnp.bfloat16)
        for ref, rels in ((near_ref, NEAR), (late_ref, LATE)):
            for i, rel in enumerate(rels):
                at = (2 * i + side) * feats
                ref[:, at : at + feats] = part[:, rel * feats : (rel + 1) * feats]


def prepare(place, grad_out, weight):
    rows, depth = grad_out.shape
    feats, width = weight.shape
    shapes = [(rows, depth // 2)] * 2 + [(width // 2, feats)] * 2
    return pl.pallas_call(
        prepare_kernel,
        grid_spec=pltpu.PrefetchScalarGridSpec(
            num_scalar_prefetch=1,
            grid=(1,),
            in_specs=[pl.BlockSpec(shape, lambda k, place: (0, 0)) for shape in (grad_out.shape, weight.shape)],
            out_specs=[pl.BlockSpec(shape, lambda k, place: (0, 0)) for shape in shapes],
        ),
        out_shape=[jax.ShapeDtypeStruct(shape, jnp.bfloat16) for shape in shapes],
        compiler_params=params(16),
        cost_estimate=pl.CostEstimate(flops=10 * rows * depth, bytes_accessed=4 * rows * depth, transcendentals=0),
        name="prepare",
    )(place, grad_out, weight)


def slab(half):
    return half // 3 if half % 48 == 0 else half


def hidden_kernel(place, gate_keep, up_keep, gate_send, up_send, keep_ref, send_ref):
    for gate_ref, up_ref, out_ref in ((gate_keep, up_keep, keep_ref), (gate_send, up_send, send_ref)):
        gate = gate_ref[...].astype(jnp.float32)
        out_ref[...] = (gate * jax.nn.sigmoid(gate) * up_ref[...].astype(jnp.float32)).astype(jnp.bfloat16)


def hidden_halves(place, gate, up):
    width, tokens = gate.shape
    rows = slab(width // 2)
    steps = width // 2 // rows
    keep_in = pl.BlockSpec((rows, tokens), lambda k, place: (place[1] * steps + k, 0))
    send_in = pl.BlockSpec((rows, tokens), lambda k, place: ((1 - place[1]) * steps + k, 0))
    block_out = pl.BlockSpec((rows, tokens), lambda k, place: (k, 0))
    out = jax.ShapeDtypeStruct((width // 2, tokens), jnp.bfloat16)
    return pl.pallas_call(
        hidden_kernel,
        grid_spec=pltpu.PrefetchScalarGridSpec(
            num_scalar_prefetch=1,
            grid=(steps,),
            in_specs=[keep_in, keep_in, send_in, send_in],
            out_specs=[block_out, block_out],
        ),
        out_shape=[out, out],
        compiler_params=params(12),
        cost_estimate=pl.CostEstimate(
            flops=6 * tokens * width, bytes_accessed=6 * tokens * width, transcendentals=2 * tokens * width
        ),
        name="hidden_halves",
    )(place, gate, up, gate, up)


def block_of(place, x_first, k, inner):
    x, y, core = place[2], 2 * place[1] + place[3], place[4] ^ (k // 4)
    way = 2 * core - 1
    dx, dy = (inner, k % 4) if x_first else (k % 4, inner)
    from_x, from_y = (x + way * dx) & 3, (y + way * dy) & 3
    return ((from_y >> 1) ^ place[1]) * 16 + from_x * 4 + (from_y & 1) * 2 + core


def fetch(place, pieces, at, slot, sem):
    (refs, starts), x_first = pieces
    rows = refs[0].shape[0] // 4
    wide = slot.shape[1]
    for dc in range(2):
        for outer in range(4):
            for inner in range(4):
                block = block_of(place, x_first, 4 * dc + outer, inner)
                to = pl.ds(pl.multiple_of(block * rows, rows), rows)
                k = 4 * dc + outer
                pltpu.make_async_copy(
                    refs[k].at[pl.ds(starts[k] + inner * rows, rows), pl.ds(at, wide)], slot.at[to, :], sem
                ).start()


def arrived(slot, sem):
    pltpu.make_async_copy(slot, slot, sem).wait()


def terms_kernel(start, starts, x_first, cut, place, keep_ref, got_ref, *refs):
    pieces, outs, slots, sems = ((refs[:8], starts), x_first), refs[8:-2], refs[-2], refs[-1]
    step, steps = pl.program_id(0), pl.num_programs(0)
    wide = slots.shape[2]
    tokens = keep_ref.shape[1]

    def bring(i):
        at = pl.multiple_of((start + i) * wide, wide)
        fetch(place, pieces, at, slots.at[lax.rem(i, 2)], sems.at[lax.rem(i, 2)])

    @pl.when(step == 0)
    def _():
        bring(step)

    @pl.when(step + 1 < steps)
    def _():
        bring(step + 1)

    now = lax.rem(step, 2)
    arrived(slots.at[now], sems.at[now])
    term = jnp.dot(keep_ref[...], slots[now, :tokens], preferred_element_type=jnp.float32) + jnp.dot(
        got_ref[...], slots[now, tokens:], preferred_element_type=jnp.float32
    )
    if cut:
        outs[0][...] = term[:cut].astype(jnp.bfloat16)
        outs[1][...] = term[cut:].astype(jnp.bfloat16)
    else:
        outs[0][0] = term.astype(jnp.bfloat16)


def batch_terms(place, keep, got, pieces, wide, start, steps, cut=0):
    half, tokens = keep.shape
    (arrays, starts), x_first = pieces
    whole = pl.BlockSpec((half, tokens), lambda k, place: (0, 0))
    if cut:
        shapes = [(cut, wide), (half - cut, wide)]
        out_shape = [jax.ShapeDtypeStruct(shape, jnp.bfloat16) for shape in shapes]
        out_specs = [pl.BlockSpec(shape, lambda k, place: (0, 0)) for shape in shapes]
    else:
        out_shape = jax.ShapeDtypeStruct((steps, half, wide), jnp.bfloat16)
        out_specs = pl.BlockSpec((1, half, wide), lambda k, place: (k, 0, 0))

    return pl.pallas_call(
        functools.partial(terms_kernel, start, starts, x_first, cut),
        grid_spec=pltpu.PrefetchScalarGridSpec(
            num_scalar_prefetch=1,
            grid=(steps,),
            in_specs=[whole, whole] + [ANYWHERE] * len(arrays),
            out_specs=out_specs,
            scratch_shapes=[pltpu.VMEM((2, 2 * tokens, wide), jnp.bfloat16), pltpu.SemaphoreType.DMA((2,))],
        ),
        out_shape=out_shape,
        compiler_params=params(20),
        name="batch_terms",
    )(place, keep, got, *arrays)


def grad_hidden_part(place, jobs, before=None):
    half, wide = jobs[-1][-1][-1][-1].shape
    rows = jobs[0][1][0].shape[0] // 4
    tokens = 16 * rows
    arrays, plans, scratch = [], [], []

    def number(array):
        for i, known in enumerate(arrays):
            if known is array:
                return i
        arrays.append(array)
        return len(arrays) - 1

    for numbers, pieces, starts, x_first, at, weights in jobs:
        plans.append(
            (
                [(k, number(piece), row) for k, piece, row in zip(numbers, pieces, starts)],
                x_first,
                at,
                [[number(part) for part in parts] for parts in weights],
            )
        )
        columns = wide * len(weights)
        scratch += [pltpu.VMEM((4 * 4 * rows, columns), jnp.bfloat16), pltpu.VMEM((half, columns), jnp.bfloat16)]
    n, last = len(arrays), before is not None

    def body(place, *refs):
        ins, rest = refs[:n], refs[n:]
        if last:
            before_ref, mine_ref, other_ref, total, *slots, sems = rest
        else:
            total, *slots, sems = rest
        for j, (pieces, x_first, at, weights) in enumerate(plans):
            slot, held = slots[2 * j], slots[2 * j + 1]
            columns = slot.shape[1]
            for i, (_, piece, row) in enumerate(pieces):
                pltpu.make_async_copy(
                    ins[piece].at[pl.ds(row, 4 * rows), pl.ds(at, columns)],
                    slot.at[pl.ds(4 * i * rows, 4 * rows), :],
                    sems.at[2 * j],
                ).start()
            for chunk, parts in enumerate(weights):
                to = 0
                for part in parts:
                    height = ins[part].shape[0]
                    pltpu.make_async_copy(
                        ins[part], held.at[pl.ds(to, height), pl.ds(chunk * wide, wide)], sems.at[2 * j + 1]
                    ).start()
                    to += height
        total[...] = before_ref[...] if last else jnp.zeros_like(total)
        for j, (pieces, x_first, at, weights) in enumerate(plans):
            slot, held = slots[2 * j], slots[2 * j + 1]
            arrived(slot, sems.at[2 * j])
            arrived(held, sems.at[2 * j + 1])
            product = lax.dot_general(
                slot[...], held[...], (((1,), (1,)), ((), ())), preferred_element_type=jnp.float32
            )
            for i in range(16):
                block = block_of(place, x_first, pieces[i // 4][0], i % 4)
                to = pl.ds(pl.multiple_of(block * rows, rows), rows)
                total[to, :] += product[i * rows : (i + 1) * rows]
        if last:
            mine_ref[...] = total[:tokens].T
            other_ref[...] = total[tokens:].T.astype(jnp.bfloat16)

    args, in_specs = list(arrays), [ANYWHERE] * n
    full = pl.BlockSpec((2 * tokens, half), lambda k, place: (0, 0))
    block = pl.BlockSpec((half, tokens), lambda k, place: (0, 0))
    scratch.append(pltpu.SemaphoreType.DMA((2 * len(jobs),)))
    if last:
        args.append(before)
        in_specs.append(full)
        scratch = [pltpu.VMEM((2 * tokens, half), jnp.float32)] + scratch
        out_specs = [block, block]
        out_shape = [
            jax.ShapeDtypeStruct((half, tokens), jnp.float32),
            jax.ShapeDtypeStruct((half, tokens), jnp.bfloat16),
        ]
    else:
        out_specs, out_shape = full, jax.ShapeDtypeStruct((2 * tokens, half), jnp.float32)
    return pl.pallas_call(
        body,
        grid_spec=pltpu.PrefetchScalarGridSpec(
            num_scalar_prefetch=1, grid=(1,), in_specs=in_specs, out_specs=out_specs, scratch_shapes=scratch
        ),
        out_shape=out_shape,
        compiler_params=params(36),
        cost_estimate=pl.CostEstimate(
            flops=sum(2 * 16 * rows * half * wide * len(job[-1]) for job in jobs), bytes_accessed=0, transcendentals=0
        ),
        name="grad_hidden",
    )(place, *args)


def gate_kernel(place, gate_ref, up_ref, grad_ref, *refs):
    grad_gate_ref, grad_up_ref = refs[-2:]
    gate = gate_ref[...].astype(jnp.float32)
    up = up_ref[...].astype(jnp.float32)
    grad_hidden = grad_ref[...].astype(jnp.float32)
    sigmoid = jax.nn.sigmoid(gate)
    grad_up_ref[...] = (grad_hidden * (gate * sigmoid)).astype(jnp.bfloat16)
    grad_gate_ref[...] = (grad_hidden * up * sigmoid * (1.0 + gate * (1.0 - sigmoid))).astype(jnp.bfloat16)


def gate_grads(place, gate, up, grad_hidden, before):
    width, tokens = gate.shape
    rows = slab(width // 2)
    steps = width // 2 // rows
    own = not before
    block = pl.BlockSpec((rows, tokens), lambda k, place: ((place[1] if own else 1 - place[1]) * steps + k, 0))
    block_half = pl.BlockSpec((rows, tokens), lambda k, place: (k, 0))
    out = jax.ShapeDtypeStruct((width, tokens), jnp.bfloat16)
    return pl.pallas_call(
        gate_kernel,
        grid_spec=pltpu.PrefetchScalarGridSpec(
            num_scalar_prefetch=1,
            grid=(steps,),
            in_specs=[block, block, block_half] + [ANYWHERE] * len(before),
            out_specs=[block, block],
        ),
        out_shape=[out, out],
        input_output_aliases={} if own else {4: 0, 5: 1},
        compiler_params=params(12),
        cost_estimate=pl.CostEstimate(
            flops=6 * tokens * width, bytes_accessed=6 * tokens * width, transcendentals=tokens * width
        ),
        name="gate_grads",
    )(place, gate, up, grad_hidden, *before)


def together(*arrays, extra=()):
    n = len(arrays)
    dtype, wide = jnp.bfloat16, [arrays[parts[0][0]].shape[1] for parts in extra]
    heights = [sum(part[2] for part in parts) for parts in extra]

    def body(*refs):
        ins, outs, sem = refs[:n], refs[2 * n : 2 * n + len(extra)], refs[-1]
        copies = []
        for parts, out in zip(extra, outs):
            to = 0
            for i, row, rows in parts:
                copies.append(
                    pltpu.make_async_copy(
                        ins[i].at[pl.ds(row, rows), :], out.at[pl.ds(to, rows), :], sem.at[len(copies)]
                    )
                )
                to += rows
        for copy in copies:
            copy.start()
        for copy in copies:
            copy.wait()

    whole = pl.BlockSpec(memory_space=pltpu.VMEM)
    count = sum(len(parts) for parts in extra)
    outs = pl.pallas_call(
        body,
        in_specs=[ANYWHERE] * n,
        out_specs=[ANYWHERE] * n + [whole] * len(extra),
        out_shape=[jax.ShapeDtypeStruct(array.shape, array.dtype) for array in arrays]
        + [jax.ShapeDtypeStruct(shape, dtype) for shape in zip(heights, wide)],
        input_output_aliases={i: i for i in range(n)},
        scratch_shapes=[pltpu.SemaphoreType.DMA((max(count, 1),))],
        compiler_params=params(4),
        name="together",
    )(*arrays)
    return outs


def lines(first, second):
    rows, wide = first[0].shape

    def body(*refs):
        for k, ref in enumerate(refs[:8]):
            part = ref[...]
            refs[8 + k // 4][k % 4 * rows : (k % 4 + 1) * rows, :] = part
            refs[10][k * rows : (k + 1) * rows, :] = part

    def block(n):
        return pl.BlockSpec((n * rows, wide), lambda: (0, 0))

    def shape(n):
        return jax.ShapeDtypeStruct((n * rows, wide), jnp.bfloat16)

    return pl.pallas_call(
        body,
        in_specs=[block(1)] * 8,
        out_specs=[block(4), block(4), block(8)],
        out_shape=[shape(4), shape(4), shape(8)],
        compiler_params=params(12),
        name="lines",
    )(*first, *second)


def pass_on(terms_up, i_up, terms_down, i_down, upward, downward):
    _, half, wide = terms_up.shape
    cut = upward.shape[0]
    whole = cut == half

    def body(up_ref, down_ref, upward_ref, downward_ref, rise_ref, fall_ref):
        def plus(a, b):
            return (a.astype(jnp.float32) + b.astype(jnp.float32)).astype(jnp.bfloat16)

        if whole:
            rise_ref[...] = plus(up_ref[0], upward_ref[...])
            fall_ref[...] = plus(down_ref[0], downward_ref[...])
        else:
            rise_ref[:cut] = plus(up_ref[0, :cut], upward_ref[...])
            rise_ref[cut:] = up_ref[0, cut:]
            fall_ref[:cut] = down_ref[0, :cut]
            fall_ref[cut:] = plus(down_ref[0, cut:], downward_ref[...])

    out = jax.ShapeDtypeStruct((half, wide), jnp.bfloat16)
    return pl.pallas_call(
        body,
        grid=(1,),
        in_specs=[
            pl.BlockSpec((1, half, wide), lambda k: (i_up, 0, 0)),
            pl.BlockSpec((1, half, wide), lambda k: (i_down, 0, 0)),
            pl.BlockSpec(upward.shape, lambda k: (0, 0)),
            pl.BlockSpec(downward.shape, lambda k: (0, 0)),
        ],
        out_specs=[pl.BlockSpec((half, wide), lambda k: (0, 0))] * 2,
        out_shape=[out, out],
        compiler_params=params(16),
        name="pass_on",
    )(terms_up, terms_down, upward, downward)


def last_sum(place, terms, i, upward, downward):
    _, half, wide = terms.shape
    feats = wide // 2

    def body(place, term_ref, upward_ref, downward_ref, keep_ref, send_ref):
        total = (
            term_ref[0].astype(jnp.float32)
            + upward_ref[...].astype(jnp.float32)
            + downward_ref[...].astype(jnp.float32)
        ).astype(jnp.bfloat16)
        first = place[1] == 0

        @pl.when(first)
        def _():
            keep_ref[...] = total[:, :feats]
            send_ref[...] = total[:, feats:]

        @pl.when(jnp.logical_not(first))
        def _():
            keep_ref[...] = total[:, feats:]
            send_ref[...] = total[:, :feats]

    out = jax.ShapeDtypeStruct((half, feats), jnp.bfloat16)
    full = pl.BlockSpec((half, wide), lambda k, place: (0, 0))
    return pl.pallas_call(
        body,
        grid_spec=pltpu.PrefetchScalarGridSpec(
            num_scalar_prefetch=1,
            grid=(1,),
            in_specs=[pl.BlockSpec((1, half, wide), lambda k, place: (i, 0, 0)), full, full],
            out_specs=[pl.BlockSpec((half, feats), lambda k, place: (0, 0))] * 2,
        ),
        out_shape=[out, out],
        compiler_params=params(16),
        name="last_sum",
    )(place, terms, upward, downward)


def local(grad_out, gate_pre, up_pre, down_weight):
    f32, bf16 = jnp.float32, jnp.bfloat16
    yh, z, x, yl, c = [lax.axis_index(name) for name in AXES]
    place = jnp.stack([z, yh, x, yl, c]).astype(jnp.int32)
    tokens, width = gate_pre.shape
    feats = down_weight.shape[0]
    half, wide = width // 2, 2 * feats
    cut = half // 32 * 16 + half % 32 // 16 * 16

    near, late, kept, leaving = prepare(place, grad_out, down_weight)
    kept_hidden, sent_hidden = hidden_halves(place, gate_pre.T, up_pre.T)

    got, near_1, late_1 = send(leaving, PARTNER), send(near, RING_Y), send(late, RING_X)
    near_3, late_3 = send(near, BACK_Y), send(late, BACK_X)
    got, near_1, late_1, near_3, late_3, sent_hidden = together(got, near_1, late_1, near_3, late_3, sent_hidden)
    pair = jnp.concatenate([jnp.where(yh == 0, kept, got), jnp.where(yh == 0, got, kept)], axis=1)

    up_1, down_1 = send(pair, along_z(1)), send(pair, along_z(-1))
    got_hidden = send(sent_hidden, PARTNER)
    near_2, late_2 = send(near_1, RING_Y), send(late_1, RING_X)
    near_0, late_0, both_0 = lines((near, near_1, near_2, near_3), (late, late_1, late_2, late_3))
    near_0, late_0, both_0, up_1, down_1, got_hidden = together(near_0, late_0, both_0, up_1, down_1, got_hidden)

    rows = near_0.shape[0]
    joint = ((2, 0, rows), (3, 0, rows))
    up_2, down_2 = send(up_1, along_z(1)), send(down_1, along_z(-1))
    near_1, late_1 = send(near_0, RING_X), send(late_0, RING_Y)
    up_2, down_2, near_1, late_1, both_0, both_1 = together(
        up_2, down_2, near_1, late_1, both_0, extra=[joint]
    )

    up_3, down_3 = send(up_2, along_z(1)), send(down_2, along_z(-1))
    near_2, late_2 = send(near_1, RING_X), send(late_1, RING_Y)
    swap_0 = send(both_0, CORES)
    up_3, down_3, near_2, late_2, swap_0, both_1, far_up, far_down = together(
        up_3, down_3, near_2, late_2, swap_0, both_1, extra=[((0, 0, cut),), ((1, cut, half - cut),)]
    )

    far_up, far_down = send(far_up, along_z(1)), send(far_down, along_z(-1))
    near_3, late_3 = send(near_2, RING_X), send(late_2, RING_Y)
    swap_1 = send(both_1, CORES)
    late_weights = [[up_2], [down_1], [up_1], [pair]]
    here = (0, 1, 2, 4)
    near_here, late_here = (near_0, near_1, near_2, swap_0), (late_0, late_1, late_2, swap_0)
    subtotal = grad_hidden_part(
        place,
        [
            (here, near_here, (0,) * 4, False, wide, [[down_3], [up_3], [down_2]]),
            (here, late_here, (0, 0, 0, rows), True, 0, late_weights),
        ],
    )
    far_up, far_down, near_3, late_3, swap_1, subtotal = together(
        far_up, far_down, near_3, late_3, swap_1, subtotal
    )

    near_swapped = [swap_0, swap_1, send(near_2, CORES), send(near_3, CORES)]
    near = ([near_0, near_1, near_2, near_3, *near_swapped], (0,) * 8), False
    late_swapped = [swap_0, swap_1, send(late_2, CORES), send(late_3, CORES)]
    late = ([late_0, late_1, late_2, late_3, *late_swapped], (0,) * 4 + (rows, rows, 0, 0)), True

    make = functools.partial(batch_terms, place, kept_hidden, got_hidden)
    farthest = make(near, wide, 0, 1, cut)
    near_terms = make(near, wide, 1, 3)
    late_first = make(late, wide, 0, 1)
    late_terms = make(late, wide, 1, 3)
    far = [far_up, far_down]
    there = (3, 5, 6, 7)
    near_there, late_there = (near_3, *near_swapped[1:]), (late_3, *late_swapped[1:])
    mine, other = grad_hidden_part(
        place,
        [
            (there, near_there, (0,) * 4, False, 0, [far, [down_3], [up_3], [down_2]]),
            (here, near_here, (0,) * 4, False, 0, [far]),
            (there, late_there, (0, rows, 0, 0), True, 0, late_weights),
        ],
        subtotal,
    )

    upward, downward = send(farthest[0], along_z(1)), send(farthest[1], along_z(-1))
    rise, fall = pass_on(near_terms, 0, near_terms, 1, upward, downward)
    upward, downward = send(rise, along_z(1)), send(fall, along_z(-1))
    upward, downward, other, late_first = together(upward, downward, other, late_first)
    got_other = send(other, PARTNER)
    rise, fall = pass_on(near_terms, 2, late_first, 0, upward, downward)
    upward, downward = send(rise, along_z(1)), send(fall, along_z(-1))
    upward, downward, got_other = together(upward, downward, got_other)
    rise, fall = pass_on(late_terms, 0, late_terms, 1, upward, downward)
    upward, downward = send(rise, along_z(1)), send(fall, along_z(-1))
    kept, leaving = last_sum(place, late_terms, 2, upward, downward)
    got = send(leaving, PARTNER)
    grad_down = jnp.concatenate([jnp.where(yh == 0, kept, got), jnp.where(yh == 0, got, kept)], axis=0).T

    grads = gate_grads(place, gate_pre.T, up_pre.T, mine, ())
    grad_gate, grad_up = gate_grads(place, gate_pre.T, up_pre.T, got_other, tuple(grads))
    return grad_gate.T, grad_up.T, grad_down


def solution(mesh):
    inner = Mesh(mesh.devices.reshape(SIZES), AXES)
    dp, tensor = ("yh", "z"), ("x", "yl", "c")
    placed = (P(dp + tensor, None), P(dp, tensor), P(dp, tensor), P(dp, tensor))
    return jax.shard_map(
        local,
        mesh=inner,
        in_specs=placed,
        out_specs=(P(dp, tensor), P(dp, tensor), P(dp, tensor)),
        check_vma=False,
    )
```

```python
import functools

import jax
import jax.numpy as jnp
from jax import lax
from jax.experimental import pallas as pl
from jax.experimental.pallas import tpu as pltpu
from jax.sharding import Mesh, PartitionSpec as P

AXES = ("yh", "z", "x", "yl", "c")
SIZES = (2, 8, 4, 2, 2)
NZ = 8
NEAR, LATE = (4, 3, 5, 2), (6, 1, 7, 0)
ANYWHERE = pl.BlockSpec(memory_space=pl.ANY)


def permutation(move):
    pairs = []
    for src in range(256):
        rest, c = divmod(src, 2)
        rest, yl = divmod(rest, 2)
        rest, x = divmod(rest, 4)
        yh, z = divmod(rest, 8)
        y, z, x, c = move(2 * yh + yl, z, x, c)
        y, z, x = y % 4, z % 8, x % 4
        dst = ((((y // 2) * 8 + z) * 4 + x) * 2 + y % 2) * 2 + c
        pairs.append((src, dst))
    return pairs


def along_z(step):
    return permutation(lambda y, z, x, c: (y, z + step, x, c))


RING_Y = permutation(lambda y, z, x, c: (y + 1 - 2 * c, z, x, c))
RING_X = permutation(lambda y, z, x, c: (y, z, x + 1 - 2 * c, c))
BACK_Y = permutation(lambda y, z, x, c: (y - 1 + 2 * c, z, x, c))
BACK_X = permutation(lambda y, z, x, c: (y, z, x - 1 + 2 * c, c))
PARTNER = permutation(lambda y, z, x, c: (y + 2, z, x, c))
CORES = permutation(lambda y, z, x, c: (y, z, x, 1 - c))


def send(value, pairs):
    return lax.ppermute(value, AXES, pairs)


def params(mib):
    return pltpu.CompilerParams(vmem_limit_bytes=mib * 2**20)


def prepare_kernel(place, grad_ref, weight_ref, near_ref, late_ref, keep_ref, send_ref):
    rows, depth = grad_ref.shape
    feats = depth // (2 * NZ)
    half = keep_ref.shape[0]
    turned = weight_ref[...].astype(jnp.float32).T.astype(jnp.bfloat16)
    first = place[1] == 0

    @pl.when(first)
    def _():
        keep_ref[...] = turned[:half]
        send_ref[...] = turned[half:]

    @pl.when(jnp.logical_not(first))
    def _():
        keep_ref[...] = turned[half:]
        send_ref[...] = turned[:half]

    shift = lax.rem((NZ - place[0]) * feats, depth // 2)
    for side in range(2):
        part = grad_ref[:, side * depth // 2 : (side + 1) * depth // 2].astype(jnp.float32)
        part = pltpu.roll(part, shift, 1).astype(jnp.bfloat16)
        for ref, rels in ((near_ref, NEAR), (late_ref, LATE)):
            for i, rel in enumerate(rels):
                at = (2 * i + side) * feats
                ref[:, at : at + feats] = part[:, rel * feats : (rel + 1) * feats]


def prepare(place, grad_out, weight):
    rows, depth = grad_out.shape
    feats, width = weight.shape
    shapes = [(rows, depth // 2)] * 2 + [(width // 2, feats)] * 2
    return pl.pallas_call(
        prepare_kernel,
        grid_spec=pltpu.PrefetchScalarGridSpec(
            num_scalar_prefetch=1,
            grid=(1,),
            in_specs=[pl.BlockSpec(shape, lambda k, place: (0, 0)) for shape in (grad_out.shape, weight.shape)],
            out_specs=[pl.BlockSpec(shape, lambda k, place: (0, 0)) for shape in shapes],
        ),
        out_shape=[jax.ShapeDtypeStruct(shape, jnp.bfloat16) for shape in shapes],
        compiler_params=params(16),
        cost_estimate=pl.CostEstimate(flops=10 * rows * depth, bytes_accessed=4 * rows * depth, transcendentals=0),
        name="prepare",
    )(place, grad_out, weight)


def slab(half):
    return half // 3 if half % 48 == 0 else half


def hidden_kernel(place, gate_keep, up_keep, gate_send, up_send, keep_ref, send_ref):
    for gate_ref, up_ref, out_ref in ((gate_keep, up_keep, keep_ref), (gate_send, up_send, send_ref)):
        gate = gate_ref[...].astype(jnp.float32)
        out_ref[...] = (gate * jax.nn.sigmoid(gate) * up_ref[...].astype(jnp.float32)).astype(jnp.bfloat16)


def hidden_halves(place, gate, up):
    width, tokens = gate.shape
    rows = slab(width // 2)
    steps = width // 2 // rows
    keep_in = pl.BlockSpec((rows, tokens), lambda k, place: (place[1] * steps + k, 0))
    send_in = pl.BlockSpec((rows, tokens), lambda k, place: ((1 - place[1]) * steps + k, 0))
    block_out = pl.BlockSpec((rows, tokens), lambda k, place: (k, 0))
    out = jax.ShapeDtypeStruct((width // 2, tokens), jnp.bfloat16)
    return pl.pallas_call(
        hidden_kernel,
        grid_spec=pltpu.PrefetchScalarGridSpec(
            num_scalar_prefetch=1,
            grid=(steps,),
            in_specs=[keep_in, keep_in, send_in, send_in],
            out_specs=[block_out, block_out],
        ),
        out_shape=[out, out],
        compiler_params=params(12),
        cost_estimate=pl.CostEstimate(
            flops=6 * tokens * width, bytes_accessed=6 * tokens * width, transcendentals=2 * tokens * width
        ),
        name="hidden_halves",
    )(place, gate, up, gate, up)


def block_of(place, x_first, k, inner):
    x, y, core = place[2], 2 * place[1] + place[3], place[4] ^ (k // 4)
    way = 2 * core - 1
    dx, dy = (inner, k % 4) if x_first else (k % 4, inner)
    from_x, from_y = (x + way * dx) & 3, (y + way * dy) & 3
    return ((from_y >> 1) ^ place[1]) * 16 + from_x * 4 + (from_y & 1) * 2 + core


def fetch(place, pieces, at, slot, sem):
    (refs, starts), x_first = pieces
    rows = refs[0].shape[0] // 4
    wide = slot.shape[1]
    for dc in range(2):
        for outer in range(4):
            for inner in range(4):
                block = block_of(place, x_first, 4 * dc + outer, inner)
                to = pl.ds(pl.multiple_of(block * rows, rows), rows)
                k = 4 * dc + outer
                pltpu.make_async_copy(
                    refs[k].at[pl.ds(starts[k] + inner * rows, rows), pl.ds(at, wide)], slot.at[to, :], sem
                ).start()


def arrived(slot, sem):
    pltpu.make_async_copy(slot, slot, sem).wait()


def terms_kernel(start, starts, x_first, cut, place, keep_ref, got_ref, *refs):
    pieces, outs, slots, sems = ((refs[:8], starts), x_first), refs[8:-2], refs[-2], refs[-1]
    step, steps = pl.program_id(0), pl.num_programs(0)
    wide = slots.shape[2]
    tokens = keep_ref.shape[1]

    def bring(i):
        at = pl.multiple_of((start + i) * wide, wide)
        fetch(place, pieces, at, slots.at[lax.rem(i, 2)], sems.at[lax.rem(i, 2)])

    @pl.when(step == 0)
    def _():
        bring(step)

    @pl.when(step + 1 < steps)
    def _():
        bring(step + 1)

    now = lax.rem(step, 2)
    arrived(slots.at[now], sems.at[now])
    term = jnp.dot(keep_ref[...], slots[now, :tokens], preferred_element_type=jnp.float32) + jnp.dot(
        got_ref[...], slots[now, tokens:], preferred_element_type=jnp.float32
    )
    if cut:
        outs[0][...] = term[:cut].astype(jnp.bfloat16)
        outs[1][...] = term[cut:].astype(jnp.bfloat16)
    else:
        outs[0][0] = term.astype(jnp.bfloat16)


def batch_terms(place, keep, got, pieces, wide, start, steps, cut=0):
    half, tokens = keep.shape
    (arrays, starts), x_first = pieces
    whole = pl.BlockSpec((half, tokens), lambda k, place: (0, 0))
    if cut:
        shapes = [(cut, wide), (half - cut, wide)]
        out_shape = [jax.ShapeDtypeStruct(shape, jnp.bfloat16) for shape in shapes]
        out_specs = [pl.BlockSpec(shape, lambda k, place: (0, 0)) for shape in shapes]
    else:
        out_shape = jax.ShapeDtypeStruct((steps, half, wide), jnp.bfloat16)
        out_specs = pl.BlockSpec((1, half, wide), lambda k, place: (k, 0, 0))

    return pl.pallas_call(
        functools.partial(terms_kernel, start, starts, x_first, cut),
        grid_spec=pltpu.PrefetchScalarGridSpec(
            num_scalar_prefetch=1,
            grid=(steps,),
            in_specs=[whole, whole] + [ANYWHERE] * len(arrays),
            out_specs=out_specs,
            scratch_shapes=[pltpu.VMEM((2, 2 * tokens, wide), jnp.bfloat16), pltpu.SemaphoreType.DMA((2,))],
        ),
        out_shape=out_shape,
        compiler_params=params(20),
        name="batch_terms",
    )(place, keep, got, *arrays)


def grad_hidden_part(place, jobs, before=None):
    half, wide = jobs[-1][-1][-1][-1].shape
    rows = jobs[0][1][0].shape[0] // 4
    tokens = 16 * rows
    arrays, plans, scratch = [], [], []

    def number(array):
        for i, known in enumerate(arrays):
            if known is array:
                return i
        arrays.append(array)
        return len(arrays) - 1

    for numbers, pieces, starts, x_first, at, weights in jobs:
        plans.append(
            (
                [(k, number(piece), row) for k, piece, row in zip(numbers, pieces, starts)],
                x_first,
                at,
                [[number(part) for part in parts] for parts in weights],
            )
        )
        columns = wide * len(weights)
        scratch += [pltpu.VMEM((4 * 4 * rows, columns), jnp.bfloat16), pltpu.VMEM((half, columns), jnp.bfloat16)]
    n, last = len(arrays), before is not None

    def body(place, *refs):
        ins, rest = refs[:n], refs[n:]
        if last:
            before_ref, mine_ref, other_ref, total, *slots, sems = rest
        else:
            total, *slots, sems = rest
        for j, (pieces, x_first, at, weights) in enumerate(plans):
            slot, held = slots[2 * j], slots[2 * j + 1]
            columns = slot.shape[1]
            for i, (_, piece, row) in enumerate(pieces):
                pltpu.make_async_copy(
                    ins[piece].at[pl.ds(row, 4 * rows), pl.ds(at, columns)],
                    slot.at[pl.ds(4 * i * rows, 4 * rows), :],
                    sems.at[2 * j],
                ).start()
            for chunk, parts in enumerate(weights):
                to = 0
                for part in parts:
                    height = ins[part].shape[0]
                    pltpu.make_async_copy(
                        ins[part], held.at[pl.ds(to, height), pl.ds(chunk * wide, wide)], sems.at[2 * j + 1]
                    ).start()
                    to += height
        total[...] = before_ref[...] if last else jnp.zeros_like(total)
        for j, (pieces, x_first, at, weights) in enumerate(plans):
            slot, held = slots[2 * j], slots[2 * j + 1]
            arrived(slot, sems.at[2 * j])
            arrived(held, sems.at[2 * j + 1])
            product = lax.dot_general(
                slot[...], held[...], (((1,), (1,)), ((), ())), preferred_element_type=jnp.float32
            )
            for i in range(16):
                block = block_of(place, x_first, pieces[i // 4][0], i % 4)
                to = pl.ds(pl.multiple_of(block * rows, rows), rows)
                total[to, :] += product[i * rows : (i + 1) * rows]
        if last:
            mine_ref[...] = total[:tokens].T
            other_ref[...] = total[tokens:].T.astype(jnp.bfloat16)

    args, in_specs = list(arrays), [ANYWHERE] * n
    full = pl.BlockSpec((2 * tokens, half), lambda k, place: (0, 0))
    block = pl.BlockSpec((half, tokens), lambda k, place: (0, 0))
    scratch.append(pltpu.SemaphoreType.DMA((2 * len(jobs),)))
    if last:
        args.append(before)
        in_specs.append(full)
        scratch = [pltpu.VMEM((2 * tokens, half), jnp.float32)] + scratch
        out_specs = [block, block]
        out_shape = [
            jax.ShapeDtypeStruct((half, tokens), jnp.float32),
            jax.ShapeDtypeStruct((half, tokens), jnp.bfloat16),
        ]
    else:
        out_specs, out_shape = full, jax.ShapeDtypeStruct((2 * tokens, half), jnp.float32)
    return pl.pallas_call(
        body,
        grid_spec=pltpu.PrefetchScalarGridSpec(
            num_scalar_prefetch=1, grid=(1,), in_specs=in_specs, out_specs=out_specs, scratch_shapes=scratch
        ),
        out_shape=out_shape,
        compiler_params=params(30),
        cost_estimate=pl.CostEstimate(
            flops=sum(2 * 16 * rows * half * wide * len(job[-1]) for job in jobs), bytes_accessed=0, transcendentals=0
        ),
        name="grad_hidden",
    )(place, *args)


def gate_kernel(place, gate_ref, up_ref, grad_ref, *refs):
    grad_gate_ref, grad_up_ref = refs[-2:]
    gate = gate_ref[...].astype(jnp.float32)
    up = up_ref[...].astype(jnp.float32)
    grad_hidden = grad_ref[...].astype(jnp.float32)
    sigmoid = jax.nn.sigmoid(gate)
    grad_up_ref[...] = (grad_hidden * (gate * sigmoid)).astype(jnp.bfloat16)
    grad_gate_ref[...] = (grad_hidden * up * sigmoid * (1.0 + gate * (1.0 - sigmoid))).astype(jnp.bfloat16)


def gate_grads(place, gate, up, grad_hidden, before):
    width, tokens = gate.shape
    rows = slab(width // 2)
    steps = width // 2 // rows
    own = not before
    block = pl.BlockSpec((rows, tokens), lambda k, place: ((place[1] if own else 1 - place[1]) * steps + k, 0))
    block_half = pl.BlockSpec((rows, tokens), lambda k, place: (k, 0))
    out = jax.ShapeDtypeStruct((width, tokens), jnp.bfloat16)
    return pl.pallas_call(
        gate_kernel,
        grid_spec=pltpu.PrefetchScalarGridSpec(
            num_scalar_prefetch=1,
            grid=(steps,),
            in_specs=[block, block, block_half] + [ANYWHERE] * len(before),
            out_specs=[block, block],
        ),
        out_shape=[out, out],
        input_output_aliases={} if own else {4: 0, 5: 1},
        compiler_params=params(12),
        cost_estimate=pl.CostEstimate(
            flops=6 * tokens * width, bytes_accessed=6 * tokens * width, transcendentals=tokens * width
        ),
        name="gate_grads",
    )(place, gate, up, grad_hidden, *before)


def together(*arrays, extra=()):
    n = len(arrays)
    dtype, wide = jnp.bfloat16, [arrays[parts[0][0]].shape[1] for parts in extra]
    heights = [sum(part[2] for part in parts) for parts in extra]

    def body(*refs):
        ins, outs, sem = refs[:n], refs[2 * n : 2 * n + len(extra)], refs[-1]
        copies = []
        for parts, out in zip(extra, outs):
            to = 0
            for i, row, rows in parts:
                copies.append(
                    pltpu.make_async_copy(
                        ins[i].at[pl.ds(row, rows), :], out.at[pl.ds(to, rows), :], sem.at[len(copies)]
                    )
                )
                to += rows
        for copy in copies:
            copy.start()
        for copy in copies:
            copy.wait()

    whole = pl.BlockSpec(memory_space=pltpu.VMEM)
    count = sum(len(parts) for parts in extra)
    outs = pl.pallas_call(
        body,
        in_specs=[ANYWHERE] * n,
        out_specs=[ANYWHERE] * n + [whole] * len(extra),
        out_shape=[jax.ShapeDtypeStruct(array.shape, array.dtype) for array in arrays]
        + [jax.ShapeDtypeStruct(shape, dtype) for shape in zip(heights, wide)],
        input_output_aliases={i: i for i in range(n)},
        scratch_shapes=[pltpu.SemaphoreType.DMA((max(count, 1),))],
        compiler_params=params(4),
        name="together",
    )(*arrays)
    return outs


def lines(first, second):
    rows, wide = first[0].shape

    def body(*refs):
        for k, ref in enumerate(refs[:8]):
            part = ref[...]
            refs[8 + k // 4][k % 4 * rows : (k % 4 + 1) * rows, :] = part
            refs[10][k * rows : (k + 1) * rows, :] = part

    def block(n):
        return pl.BlockSpec((n * rows, wide), lambda: (0, 0))

    def shape(n):
        return jax.ShapeDtypeStruct((n * rows, wide), jnp.bfloat16)

    return pl.pallas_call(
        body,
        in_specs=[block(1)] * 8,
        out_specs=[block(4), block(4), block(8)],
        out_shape=[shape(4), shape(4), shape(8)],
        compiler_params=params(12),
        name="lines",
    )(*first, *second)


def pass_on(terms_up, i_up, terms_down, i_down, upward, downward):
    _, half, wide = terms_up.shape
    cut = upward.shape[0]
    whole = cut == half

    def body(up_ref, down_ref, upward_ref, downward_ref, rise_ref, fall_ref):
        def plus(a, b):
            return (a.astype(jnp.float32) + b.astype(jnp.float32)).astype(jnp.bfloat16)

        if whole:
            rise_ref[...] = plus(up_ref[0], upward_ref[...])
            fall_ref[...] = plus(down_ref[0], downward_ref[...])
        else:
            rise_ref[:cut] = plus(up_ref[0, :cut], upward_ref[...])
            rise_ref[cut:] = up_ref[0, cut:]
            fall_ref[:cut] = down_ref[0, :cut]
            fall_ref[cut:] = plus(down_ref[0, cut:], downward_ref[...])

    out = jax.ShapeDtypeStruct((half, wide), jnp.bfloat16)
    return pl.pallas_call(
        body,
        grid=(1,),
        in_specs=[
            pl.BlockSpec((1, half, wide), lambda k: (i_up, 0, 0)),
            pl.BlockSpec((1, half, wide), lambda k: (i_down, 0, 0)),
            pl.BlockSpec(upward.shape, lambda k: (0, 0)),
            pl.BlockSpec(downward.shape, lambda k: (0, 0)),
        ],
        out_specs=[pl.BlockSpec((half, wide), lambda k: (0, 0))] * 2,
        out_shape=[out, out],
        compiler_params=params(16),
        name="pass_on",
    )(terms_up, terms_down, upward, downward)


def pass_halves(terms, i_up, i_down, upward, downward, cut):
    _, half, wide = terms.shape

    def body(up_ref, down_ref, upward_ref, downward_ref, *outs):
        for term_ref, sum_ref, (low, high) in ((up_ref, upward_ref, outs[:2]), (down_ref, downward_ref, outs[2:])):
            total = (term_ref[0].astype(jnp.float32) + sum_ref[...].astype(jnp.float32)).astype(jnp.bfloat16)
            low[...] = total[:cut]
            high[...] = total[cut:]

    full = pl.BlockSpec((half, wide), lambda k: (0, 0))
    shapes = [(cut, wide), (half - cut, wide)] * 2
    return pl.pallas_call(
        body,
        grid=(1,),
        in_specs=[
            pl.BlockSpec((1, half, wide), lambda k: (i_up, 0, 0)),
            pl.BlockSpec((1, half, wide), lambda k: (i_down, 0, 0)),
            full,
            full,
        ],
        out_specs=[pl.BlockSpec(shape, lambda k: (0, 0)) for shape in shapes],
        out_shape=[jax.ShapeDtypeStruct(shape, jnp.bfloat16) for shape in shapes],
        compiler_params=params(16),
        name="pass_halves",
    )(terms, terms, upward, downward)


def last_sum(place, terms, i, row, upward, downward, after):
    _, half, wide = terms.shape
    rows = upward.shape[0]
    feats = wide // 2

    def body(place, term_ref, upward_ref, downward_ref, *refs):
        keep_ref, send_ref = refs[-2:]
        total = (
            term_ref[0, row : row + rows].astype(jnp.float32)
            + upward_ref[...].astype(jnp.float32)
            + downward_ref[...].astype(jnp.float32)
        ).astype(jnp.bfloat16)
        first = place[1] == 0

        @pl.when(first)
        def _():
            keep_ref[...] = total[:, :feats]
            send_ref[...] = total[:, feats:]

        @pl.when(jnp.logical_not(first))
        def _():
            keep_ref[...] = total[:, feats:]
            send_ref[...] = total[:, :feats]

    out = jax.ShapeDtypeStruct((rows, feats), jnp.bfloat16)
    part = pl.BlockSpec((rows, wide), lambda k, place: (0, 0))
    return pl.pallas_call(
        body,
        grid_spec=pltpu.PrefetchScalarGridSpec(
            num_scalar_prefetch=1,
            grid=(1,),
            in_specs=[pl.BlockSpec((1, half, wide), lambda k, place: (i, 0, 0)), part, part] + [ANYWHERE] * len(after),
            out_specs=[pl.BlockSpec((rows, feats), lambda k, place: (0, 0))] * 2,
        ),
        out_shape=[out, out],
        compiler_params=params(16),
        name="last_sum",
    )(place, terms, upward, downward, *after)


def local(grad_out, gate_pre, up_pre, down_weight):
    f32, bf16 = jnp.float32, jnp.bfloat16
    yh, z, x, yl, c = [lax.axis_index(name) for name in AXES]
    place = jnp.stack([z, yh, x, yl, c]).astype(jnp.int32)
    tokens, width = gate_pre.shape
    feats = down_weight.shape[0]
    half, wide = width // 2, 2 * feats
    cut = half // 32 * 16 + half % 32 // 16 * 16

    near, late, kept, leaving = prepare(place, grad_out, down_weight)
    kept_hidden, sent_hidden = hidden_halves(place, gate_pre.T, up_pre.T)

    got, near_1, late_1 = send(leaving, PARTNER), send(near, RING_Y), send(late, RING_X)
    near_3, late_3 = send(near, BACK_Y), send(late, BACK_X)
    got, near_1, late_1, near_3, late_3, sent_hidden = together(got, near_1, late_1, near_3, late_3, sent_hidden)
    pair = jnp.concatenate([jnp.where(yh == 0, kept, got), jnp.where(yh == 0, got, kept)], axis=1)

    up_1, down_1 = send(pair, along_z(1)), send(pair, along_z(-1))
    got_hidden = send(sent_hidden, PARTNER)
    near_2, late_2 = send(near_1, RING_Y), send(late_1, RING_X)
    near_0, late_0, both_0 = lines((near, near_1, near_2, near_3), (late, late_1, late_2, late_3))
    near_0, late_0, both_0, up_1, down_1, got_hidden = together(near_0, late_0, both_0, up_1, down_1, got_hidden)

    rows = near_0.shape[0]
    joint = ((2, 0, rows), (3, 0, rows))
    up_2, down_2 = send(up_1, along_z(1)), send(down_1, along_z(-1))
    near_1, late_1 = send(near_0, RING_X), send(late_0, RING_Y)
    up_2, down_2, near_1, late_1, both_0, both_1 = together(
        up_2, down_2, near_1, late_1, both_0, extra=[joint]
    )

    up_3, down_3 = send(up_2, along_z(1)), send(down_2, along_z(-1))
    near_2, late_2 = send(near_1, RING_X), send(late_1, RING_Y)
    swap_0 = send(both_0, CORES)
    up_3, down_3, near_2, late_2, swap_0, both_1, far_up, far_down = together(
        up_3, down_3, near_2, late_2, swap_0, both_1, extra=[((0, 0, cut),), ((1, cut, half - cut),)]
    )

    far_up, far_down = send(far_up, along_z(1)), send(far_down, along_z(-1))
    near_3, late_3 = send(near_2, RING_X), send(late_2, RING_Y)
    swap_1 = send(both_1, CORES)
    late_weights = [[up_2], [down_1], [up_1], [pair]]
    here = (0, 1, 2, 4)
    near_here, late_here = (near_0, near_1, near_2, swap_0), (late_0, late_1, late_2, swap_0)
    subtotal = grad_hidden_part(
        place,
        [
            (here, near_here, (0,) * 4, False, wide, [[down_3], [up_3], [down_2]]),
            (here, late_here, (0, 0, 0, rows), True, 0, late_weights),
        ],
    )
    far_up, far_down, near_3, late_3, swap_1, subtotal = together(
        far_up, far_down, near_3, late_3, swap_1, subtotal
    )

    near_swapped = [swap_0, swap_1, send(near_2, CORES), send(near_3, CORES)]
    near = ([near_0, near_1, near_2, near_3, *near_swapped], (0,) * 8), False
    late_swapped = [swap_0, swap_1, send(late_2, CORES), send(late_3, CORES)]
    late = ([late_0, late_1, late_2, late_3, *late_swapped], (0,) * 4 + (rows, rows, 0, 0)), True

    make = functools.partial(batch_terms, place, kept_hidden, got_hidden)
    farthest = make(near, wide, 0, 1, cut)
    near_terms = make(near, wide, 1, 3)
    late_first = make(late, wide, 0, 1)
    late_terms = make(late, wide, 1, 3)
    far = [far_up, far_down]
    there = (3, 5, 6, 7)
    near_there, late_there = (near_3, *near_swapped[1:]), (late_3, *late_swapped[1:])
    mine, other = grad_hidden_part(
        place,
        [
            (there, near_there, (0,) * 4, False, 0, [far, [down_3], [up_3], [down_2]]),
            (here, near_here, (0,) * 4, False, 0, [far]),
            (there, late_there, (0, rows, 0, 0), True, 0, late_weights),
        ],
        subtotal,
    )

    upward, downward = send(farthest[0], along_z(1)), send(farthest[1], along_z(-1))
    rise, fall = pass_on(near_terms, 0, near_terms, 1, upward, downward)
    upward, downward = send(rise, along_z(1)), send(fall, along_z(-1))
    upward, downward, other, late_first = together(upward, downward, other, late_first)
    got_other = send(other, PARTNER)
    rise, fall = pass_on(near_terms, 2, late_first, 0, upward, downward)
    upward, downward = send(rise, along_z(1)), send(fall, along_z(-1))
    grads = gate_grads(place, gate_pre.T, up_pre.T, mine, ())
    upward, downward, got_other, *grads = together(upward, downward, got_other, *grads)
    rise, rise_high, fall, fall_high = pass_halves(late_terms, 0, 1, upward, downward, cut)
    kept, got = [], []
    for row, up, down in ((0, rise, fall), (cut, rise_high, fall_high)):
        up, down = send(up, along_z(1)), send(down, along_z(-1))
        own, leaving = last_sum(place, late_terms, 2, row, up, down, kept)
        kept.append(own)
        got.append(send(leaving, PARTNER))
    kept, got = jnp.concatenate(kept, axis=0), jnp.concatenate(got, axis=0)
    grad_down = jnp.concatenate([jnp.where(yh == 0, kept, got), jnp.where(yh == 0, got, kept)], axis=0).T

    grad_gate, grad_up = gate_grads(place, gate_pre.T, up_pre.T, got_other, tuple(grads))
    return grad_gate.T, grad_up.T, grad_down


def solution(mesh):
    inner = Mesh(mesh.devices.reshape(SIZES), AXES)
    dp, tensor = ("yh", "z"), ("x", "yl", "c")
    placed = (P(dp + tensor, None), P(dp, tensor), P(dp, tensor), P(dp, tensor))
    return jax.shard_map(
        local,
        mesh=inner,
        in_specs=placed,
        out_specs=(P(dp, tensor), P(dp, tensor), P(dp, tensor)),
        check_vma=False,
    )
```

```python
import functools

import jax
import jax.numpy as jnp
from jax import lax
from jax.experimental import pallas as pl
from jax.experimental.pallas import tpu as pltpu
from jax.sharding import Mesh, PartitionSpec as P

AXES = ("yh", "z", "x", "yl", "c")
SIZES = (2, 8, 4, 2, 2)
NZ = 8
NEAR, LATE = (4, 3, 5, 2), (6, 1, 7, 0)
ANYWHERE = pl.BlockSpec(memory_space=pl.ANY)


def permutation(move):
    pairs = []
    for src in range(256):
        rest, c = divmod(src, 2)
        rest, yl = divmod(rest, 2)
        rest, x = divmod(rest, 4)
        yh, z = divmod(rest, 8)
        y, z, x, c = move(2 * yh + yl, z, x, c)
        y, z, x = y % 4, z % 8, x % 4
        dst = ((((y // 2) * 8 + z) * 4 + x) * 2 + y % 2) * 2 + c
        pairs.append((src, dst))
    return pairs


def along_z(step):
    return permutation(lambda y, z, x, c: (y, z + step, x, c))


RING_Y = permutation(lambda y, z, x, c: (y + 1 - 2 * c, z, x, c))
RING_X = permutation(lambda y, z, x, c: (y, z, x + 1 - 2 * c, c))
BACK_Y = permutation(lambda y, z, x, c: (y - 1 + 2 * c, z, x, c))
BACK_X = permutation(lambda y, z, x, c: (y, z, x - 1 + 2 * c, c))
PARTNER = permutation(lambda y, z, x, c: (y + 2, z, x, c))
CORES = permutation(lambda y, z, x, c: (y, z, x, 1 - c))


def send(value, pairs):
    return lax.ppermute(value, AXES, pairs)


def params(mib):
    return pltpu.CompilerParams(vmem_limit_bytes=mib * 2**20)


def prepare_kernel(place, grad_ref, weight_ref, near_ref, late_ref, keep_ref, send_ref):
    rows, depth = grad_ref.shape
    feats = depth // (2 * NZ)
    half = keep_ref.shape[0]
    turned = weight_ref[...].astype(jnp.float32).T.astype(jnp.bfloat16)
    first = place[1] == 0

    @pl.when(first)
    def _():
        keep_ref[...] = turned[:half]
        send_ref[...] = turned[half:]

    @pl.when(jnp.logical_not(first))
    def _():
        keep_ref[...] = turned[half:]
        send_ref[...] = turned[:half]

    shift = lax.rem((NZ - place[0]) * feats, depth // 2)
    for side in range(2):
        part = grad_ref[:, side * depth // 2 : (side + 1) * depth // 2].astype(jnp.float32)
        part = pltpu.roll(part, shift, 1).astype(jnp.bfloat16)
        for ref, rels in ((near_ref, NEAR), (late_ref, LATE)):
            for i, rel in enumerate(rels):
                at = (2 * i + side) * feats
                ref[:, at : at + feats] = part[:, rel * feats : (rel + 1) * feats]


def prepare(place, grad_out, weight):
    rows, depth = grad_out.shape
    feats, width = weight.shape
    shapes = [(rows, depth // 2)] * 2 + [(width // 2, feats)] * 2
    return pl.pallas_call(
        prepare_kernel,
        grid_spec=pltpu.PrefetchScalarGridSpec(
            num_scalar_prefetch=1,
            grid=(1,),
            in_specs=[pl.BlockSpec(shape, lambda k, place: (0, 0)) for shape in (grad_out.shape, weight.shape)],
            out_specs=[pl.BlockSpec(shape, lambda k, place: (0, 0)) for shape in shapes],
        ),
        out_shape=[jax.ShapeDtypeStruct(shape, jnp.bfloat16) for shape in shapes],
        compiler_params=params(16),
        cost_estimate=pl.CostEstimate(flops=10 * rows * depth, bytes_accessed=4 * rows * depth, transcendentals=0),
        name="prepare",
    )(place, grad_out, weight)


def slab(half):
    return half // 3 if half % 48 == 0 else half


def hidden_kernel(place, gate_keep, up_keep, gate_send, up_send, keep_ref, send_ref):
    for gate_ref, up_ref, out_ref in ((gate_keep, up_keep, keep_ref), (gate_send, up_send, send_ref)):
        gate = gate_ref[...].astype(jnp.float32)
        out_ref[...] = (gate * jax.nn.sigmoid(gate) * up_ref[...].astype(jnp.float32)).astype(jnp.bfloat16)


def hidden_halves(place, gate, up):
    width, tokens = gate.shape
    rows = slab(width // 2)
    steps = width // 2 // rows
    keep_in = pl.BlockSpec((rows, tokens), lambda k, place: (place[1] * steps + k, 0))
    send_in = pl.BlockSpec((rows, tokens), lambda k, place: ((1 - place[1]) * steps + k, 0))
    block_out = pl.BlockSpec((rows, tokens), lambda k, place: (k, 0))
    out = jax.ShapeDtypeStruct((width // 2, tokens), jnp.bfloat16)
    return pl.pallas_call(
        hidden_kernel,
        grid_spec=pltpu.PrefetchScalarGridSpec(
            num_scalar_prefetch=1,
            grid=(steps,),
            in_specs=[keep_in, keep_in, send_in, send_in],
            out_specs=[block_out, block_out],
        ),
        out_shape=[out, out],
        compiler_params=params(12),
        cost_estimate=pl.CostEstimate(
            flops=6 * tokens * width, bytes_accessed=6 * tokens * width, transcendentals=2 * tokens * width
        ),
        name="hidden_halves",
    )(place, gate, up, gate, up)


def block_of(place, x_first, k, inner):
    x, y, core = place[2], 2 * place[1] + place[3], place[4] ^ (k // 4)
    way = 2 * core - 1
    dx, dy = (inner, k % 4) if x_first else (k % 4, inner)
    from_x, from_y = (x + way * dx) & 3, (y + way * dy) & 3
    return ((from_y >> 1) ^ place[1]) * 16 + from_x * 4 + (from_y & 1) * 2 + core


def fetch(place, pieces, at, slot, sem):
    (refs, starts), x_first = pieces
    rows = refs[0].shape[0] // 4
    wide = slot.shape[1]
    for dc in range(2):
        for outer in range(4):
            for inner in range(4):
                block = block_of(place, x_first, 4 * dc + outer, inner)
                to = pl.ds(pl.multiple_of(block * rows, rows), rows)
                k = 4 * dc + outer
                pltpu.make_async_copy(
                    refs[k].at[pl.ds(starts[k] + inner * rows, rows), pl.ds(at, wide)], slot.at[to, :], sem
                ).start()


def arrived(slot, sem):
    pltpu.make_async_copy(slot, slot, sem).wait()


def terms_kernel(start, starts, x_first, cut, place, keep_ref, got_ref, *refs):
    pieces, outs, slots, sems = ((refs[:8], starts), x_first), refs[8:-2], refs[-2], refs[-1]
    step, steps = pl.program_id(0), pl.num_programs(0)
    wide = slots.shape[2]
    tokens = keep_ref.shape[1]

    def bring(i):
        at = pl.multiple_of((start + i) * wide, wide)
        fetch(place, pieces, at, slots.at[lax.rem(i, 2)], sems.at[lax.rem(i, 2)])

    @pl.when(step == 0)
    def _():
        bring(step)

    @pl.when(step + 1 < steps)
    def _():
        bring(step + 1)

    now = lax.rem(step, 2)
    arrived(slots.at[now], sems.at[now])
    term = jnp.dot(keep_ref[...], slots[now, :tokens], preferred_element_type=jnp.float32) + jnp.dot(
        got_ref[...], slots[now, tokens:], preferred_element_type=jnp.float32
    )
    if cut:
        outs[0][...] = term[:cut].astype(jnp.bfloat16)
        outs[1][...] = term[cut:].astype(jnp.bfloat16)
    else:
        outs[0][0] = term.astype(jnp.bfloat16)


def batch_terms(place, keep, got, pieces, wide, start, steps, cut=0):
    half, tokens = keep.shape
    (arrays, starts), x_first = pieces
    whole = pl.BlockSpec((half, tokens), lambda k, place: (0, 0))
    if cut:
        shapes = [(cut, wide), (half - cut, wide)]
        out_shape = [jax.ShapeDtypeStruct(shape, jnp.bfloat16) for shape in shapes]
        out_specs = [pl.BlockSpec(shape, lambda k, place: (0, 0)) for shape in shapes]
    else:
        out_shape = jax.ShapeDtypeStruct((steps, half, wide), jnp.bfloat16)
        out_specs = pl.BlockSpec((1, half, wide), lambda k, place: (k, 0, 0))

    return pl.pallas_call(
        functools.partial(terms_kernel, start, starts, x_first, cut),
        grid_spec=pltpu.PrefetchScalarGridSpec(
            num_scalar_prefetch=1,
            grid=(steps,),
            in_specs=[whole, whole] + [ANYWHERE] * len(arrays),
            out_specs=out_specs,
            scratch_shapes=[pltpu.VMEM((2, 2 * tokens, wide), jnp.bfloat16), pltpu.SemaphoreType.DMA((2,))],
        ),
        out_shape=out_shape,
        compiler_params=params(20),
        name="batch_terms",
    )(place, keep, got, *arrays)


def grad_hidden_part(place, jobs, before=None):
    half, wide = jobs[-1][-1][-1][-1].shape
    rows = jobs[0][1][0].shape[0] // 4
    tokens = 16 * rows
    arrays, plans, scratch = [], [], []

    def number(array):
        for i, known in enumerate(arrays):
            if known is array:
                return i
        arrays.append(array)
        return len(arrays) - 1

    for numbers, pieces, starts, x_first, at, weights in jobs:
        plans.append(
            (
                [(k, number(piece), row) for k, piece, row in zip(numbers, pieces, starts)],
                x_first,
                at,
                [[number(part) for part in parts] for parts in weights],
            )
        )
        columns = wide * len(weights)
        scratch += [pltpu.VMEM((4 * 4 * rows, columns), jnp.bfloat16), pltpu.VMEM((half, columns), jnp.bfloat16)]
    n, last = len(arrays), before is not None

    def body(place, *refs):
        ins, rest = refs[:n], refs[n:]
        if last:
            before_ref, mine_ref, other_ref, total, *slots, sems = rest
        else:
            total, *slots, sems = rest
        for j, (pieces, x_first, at, weights) in enumerate(plans):
            slot, held = slots[2 * j], slots[2 * j + 1]
            columns = slot.shape[1]
            for i, (_, piece, row) in enumerate(pieces):
                pltpu.make_async_copy(
                    ins[piece].at[pl.ds(row, 4 * rows), pl.ds(at, columns)],
                    slot.at[pl.ds(4 * i * rows, 4 * rows), :],
                    sems.at[2 * j],
                ).start()
            for chunk, parts in enumerate(weights):
                to = 0
                for part in parts:
                    height = ins[part].shape[0]
                    pltpu.make_async_copy(
                        ins[part], held.at[pl.ds(to, height), pl.ds(chunk * wide, wide)], sems.at[2 * j + 1]
                    ).start()
                    to += height
        total[...] = before_ref[...] if last else jnp.zeros_like(total)
        for j, (pieces, x_first, at, weights) in enumerate(plans):
            slot, held = slots[2 * j], slots[2 * j + 1]
            arrived(slot, sems.at[2 * j])
            arrived(held, sems.at[2 * j + 1])
            product = lax.dot_general(
                slot[...], held[...], (((1,), (1,)), ((), ())), preferred_element_type=jnp.float32
            )
            for i in range(16):
                block = block_of(place, x_first, pieces[i // 4][0], i % 4)
                to = pl.ds(pl.multiple_of(block * rows, rows), rows)
                total[to, :] += product[i * rows : (i + 1) * rows]
        if last:
            mine_ref[...] = total[:tokens].T
            other_ref[...] = total[tokens:].T.astype(jnp.bfloat16)

    args, in_specs = list(arrays), [ANYWHERE] * n
    full = pl.BlockSpec((2 * tokens, half), lambda k, place: (0, 0))
    block = pl.BlockSpec((half, tokens), lambda k, place: (0, 0))
    scratch.append(pltpu.SemaphoreType.DMA((2 * len(jobs),)))
    if last:
        args.append(before)
        in_specs.append(full)
        scratch = [pltpu.VMEM((2 * tokens, half), jnp.float32)] + scratch
        out_specs = [block, block]
        out_shape = [
            jax.ShapeDtypeStruct((half, tokens), jnp.float32),
            jax.ShapeDtypeStruct((half, tokens), jnp.bfloat16),
        ]
    else:
        out_specs, out_shape = full, jax.ShapeDtypeStruct((2 * tokens, half), jnp.float32)
    return pl.pallas_call(
        body,
        grid_spec=pltpu.PrefetchScalarGridSpec(
            num_scalar_prefetch=1, grid=(1,), in_specs=in_specs, out_specs=out_specs, scratch_shapes=scratch
        ),
        out_shape=out_shape,
        compiler_params=params(30),
        cost_estimate=pl.CostEstimate(
            flops=sum(2 * 16 * rows * half * wide * len(job[-1]) for job in jobs), bytes_accessed=0, transcendentals=0
        ),
        name="grad_hidden",
    )(place, *args)


def gate_kernel(place, gate_ref, up_ref, grad_ref, *refs):
    grad_gate_ref, grad_up_ref = refs[-2:]
    gate = gate_ref[...].astype(jnp.float32)
    up = up_ref[...].astype(jnp.float32)
    grad_hidden = grad_ref[...].astype(jnp.float32)
    sigmoid = jax.nn.sigmoid(gate)
    grad_up_ref[...] = (grad_hidden * (gate * sigmoid)).astype(jnp.bfloat16)
    grad_gate_ref[...] = (grad_hidden * up * sigmoid * (1.0 + gate * (1.0 - sigmoid))).astype(jnp.bfloat16)


def gate_grads(place, gate, up, grad_hidden, before):
    width, tokens = gate.shape
    rows = slab(width // 2)
    steps = width // 2 // rows
    own = not before
    block = pl.BlockSpec((rows, tokens), lambda k, place: ((place[1] if own else 1 - place[1]) * steps + k, 0))
    block_half = pl.BlockSpec((rows, tokens), lambda k, place: (k, 0))
    out = jax.ShapeDtypeStruct((width, tokens), jnp.bfloat16)
    return pl.pallas_call(
        gate_kernel,
        grid_spec=pltpu.PrefetchScalarGridSpec(
            num_scalar_prefetch=1,
            grid=(steps,),
            in_specs=[block, block, block_half] + [ANYWHERE] * len(before),
            out_specs=[block, block],
        ),
        out_shape=[out, out],
        input_output_aliases={} if own else {4: 0, 5: 1},
        compiler_params=params(12),
        cost_estimate=pl.CostEstimate(
            flops=6 * tokens * width, bytes_accessed=6 * tokens * width, transcendentals=tokens * width
        ),
        name="gate_grads",
    )(place, gate, up, grad_hidden, *before)


def together(*arrays, extra=()):
    n = len(arrays)
    dtype, wide = jnp.bfloat16, [arrays[parts[0][0]].shape[1] for parts in extra]
    heights = [sum(part[2] for part in parts) for parts in extra]

    def body(*refs):
        ins, outs, sem = refs[:n], refs[2 * n : 2 * n + len(extra)], refs[-1]
        copies = []
        for parts, out in zip(extra, outs):
            to = 0
            for i, row, rows in parts:
                copies.append(
                    pltpu.make_async_copy(
                        ins[i].at[pl.ds(row, rows), :], out.at[pl.ds(to, rows), :], sem.at[len(copies)]
                    )
                )
                to += rows
        for copy in copies:
            copy.start()
        for copy in copies:
            copy.wait()

    whole = pl.BlockSpec(memory_space=pltpu.VMEM)
    count = sum(len(parts) for parts in extra)
    outs = pl.pallas_call(
        body,
        in_specs=[ANYWHERE] * n,
        out_specs=[ANYWHERE] * n + [whole] * len(extra),
        out_shape=[jax.ShapeDtypeStruct(array.shape, array.dtype) for array in arrays]
        + [jax.ShapeDtypeStruct(shape, dtype) for shape in zip(heights, wide)],
        input_output_aliases={i: i for i in range(n)},
        scratch_shapes=[pltpu.SemaphoreType.DMA((max(count, 1),))],
        compiler_params=params(4),
        name="together",
    )(*arrays)
    return outs


def lines(first, second):
    rows, wide = first[0].shape

    def body(*refs):
        for k, ref in enumerate(refs[:8]):
            part = ref[...]
            refs[8 + k // 4][k % 4 * rows : (k % 4 + 1) * rows, :] = part
            refs[10][k * rows : (k + 1) * rows, :] = part

    def block(n):
        return pl.BlockSpec((n * rows, wide), lambda: (0, 0))

    def shape(n):
        return jax.ShapeDtypeStruct((n * rows, wide), jnp.bfloat16)

    return pl.pallas_call(
        body,
        in_specs=[block(1)] * 8,
        out_specs=[block(4), block(4), block(8)],
        out_shape=[shape(4), shape(4), shape(8)],
        compiler_params=params(12),
        name="lines",
    )(*first, *second)


def pass_on(terms_up, i_up, terms_down, i_down, upward, downward):
    _, half, wide = terms_up.shape
    cut = upward.shape[0]
    whole = cut == half

    def body(up_ref, down_ref, upward_ref, downward_ref, rise_ref, fall_ref):
        def plus(a, b):
            return (a.astype(jnp.float32) + b.astype(jnp.float32)).astype(jnp.bfloat16)

        if whole:
            rise_ref[...] = plus(up_ref[0], upward_ref[...])
            fall_ref[...] = plus(down_ref[0], downward_ref[...])
        else:
            rise_ref[:cut] = plus(up_ref[0, :cut], upward_ref[...])
            rise_ref[cut:] = up_ref[0, cut:]
            fall_ref[:cut] = down_ref[0, :cut]
            fall_ref[cut:] = plus(down_ref[0, cut:], downward_ref[...])

    out = jax.ShapeDtypeStruct((half, wide), jnp.bfloat16)
    return pl.pallas_call(
        body,
        grid=(1,),
        in_specs=[
            pl.BlockSpec((1, half, wide), lambda k: (i_up, 0, 0)),
            pl.BlockSpec((1, half, wide), lambda k: (i_down, 0, 0)),
            pl.BlockSpec(upward.shape, lambda k: (0, 0)),
            pl.BlockSpec(downward.shape, lambda k: (0, 0)),
        ],
        out_specs=[pl.BlockSpec((half, wide), lambda k: (0, 0))] * 2,
        out_shape=[out, out],
        compiler_params=params(16),
        name="pass_on",
    )(terms_up, terms_down, upward, downward)


def pass_halves(terms, i_up, i_down, upward, downward, cut):
    _, half, wide = terms.shape

    def body(up_ref, down_ref, upward_ref, downward_ref, *outs):
        for term_ref, sum_ref, (low, high) in ((up_ref, upward_ref, outs[:2]), (down_ref, downward_ref, outs[2:])):
            total = (term_ref[0].astype(jnp.float32) + sum_ref[...].astype(jnp.float32)).astype(jnp.bfloat16)
            low[...] = total[:cut]
            high[...] = total[cut:]

    full = pl.BlockSpec((half, wide), lambda k: (0, 0))
    shapes = [(cut, wide), (half - cut, wide)] * 2
    return pl.pallas_call(
        body,
        grid=(1,),
        in_specs=[
            pl.BlockSpec((1, half, wide), lambda k: (i_up, 0, 0)),
            pl.BlockSpec((1, half, wide), lambda k: (i_down, 0, 0)),
            full,
            full,
        ],
        out_specs=[pl.BlockSpec(shape, lambda k: (0, 0)) for shape in shapes],
        out_shape=[jax.ShapeDtypeStruct(shape, jnp.bfloat16) for shape in shapes],
        compiler_params=params(16),
        name="pass_halves",
    )(terms, terms, upward, downward)


def last_sum(place, terms, i, row, upward, downward, after):
    _, half, wide = terms.shape
    rows = upward.shape[0]
    feats = wide // 2

    def body(place, term_ref, upward_ref, downward_ref, *refs):
        keep_ref, send_ref = refs[-2:]
        total = (
            term_ref[0, row : row + rows].astype(jnp.float32)
            + upward_ref[...].astype(jnp.float32)
            + downward_ref[...].astype(jnp.float32)
        ).astype(jnp.bfloat16)
        first = place[1] == 0

        @pl.when(first)
        def _():
            keep_ref[...] = total[:, :feats]
            send_ref[...] = total[:, feats:]

        @pl.when(jnp.logical_not(first))
        def _():
            keep_ref[...] = total[:, feats:]
            send_ref[...] = total[:, :feats]

    out = jax.ShapeDtypeStruct((rows, feats), jnp.bfloat16)
    part = pl.BlockSpec((rows, wide), lambda k, place: (0, 0))
    return pl.pallas_call(
        body,
        grid_spec=pltpu.PrefetchScalarGridSpec(
            num_scalar_prefetch=1,
            grid=(1,),
            in_specs=[pl.BlockSpec((1, half, wide), lambda k, place: (i, 0, 0)), part, part] + [ANYWHERE] * len(after),
            out_specs=[pl.BlockSpec((rows, feats), lambda k, place: (0, 0))] * 2,
        ),
        out_shape=[out, out],
        compiler_params=params(16),
        name="last_sum",
    )(place, terms, upward, downward, *after)


def local(grad_out, gate_pre, up_pre, down_weight):
    f32, bf16 = jnp.float32, jnp.bfloat16
    yh, z, x, yl, c = [lax.axis_index(name) for name in AXES]
    place = jnp.stack([z, yh, x, yl, c]).astype(jnp.int32)
    tokens, width = gate_pre.shape
    feats = down_weight.shape[0]
    half, wide = width // 2, 2 * feats
    cut = half // 32 * 16 + half % 32 // 16 * 16

    near, late, kept, leaving = prepare(place, grad_out, down_weight)
    kept_hidden, sent_hidden = hidden_halves(place, gate_pre.T, up_pre.T)

    got, near_1, late_1 = send(leaving, PARTNER), send(near, RING_Y), send(late, RING_X)
    near_3, late_3 = send(near, BACK_Y), send(late, BACK_X)
    got, near_1, late_1, near_3, late_3, sent_hidden = together(got, near_1, late_1, near_3, late_3, sent_hidden)
    pair = jnp.concatenate([jnp.where(yh == 0, kept, got), jnp.where(yh == 0, got, kept)], axis=1)

    up_1, down_1 = send(pair, along_z(1)), send(pair, along_z(-1))
    got_hidden = send(sent_hidden, PARTNER)
    near_2, late_2 = send(near_1, RING_Y), send(late_1, RING_X)
    near_0, late_0, both_0 = lines((near, near_1, near_2, near_3), (late, late_1, late_2, late_3))
    near_0, late_0, both_0, up_1, down_1, got_hidden = together(near_0, late_0, both_0, up_1, down_1, got_hidden)

    rows = near_0.shape[0]
    joint = ((2, 0, rows), (3, 0, rows))
    up_2, down_2 = send(up_1, along_z(1)), send(down_1, along_z(-1))
    near_1, late_1 = send(near_0, RING_X), send(late_0, RING_Y)
    swap_0 = send(both_0, CORES)
    up_2, down_2, near_1, late_1, swap_0, both_1 = together(
        up_2, down_2, near_1, late_1, swap_0, extra=[joint]
    )

    up_3, down_3 = send(up_2, along_z(1)), send(down_2, along_z(-1))
    near_2, late_2 = send(near_1, RING_X), send(late_1, RING_Y)
    swap_1 = send(both_1, CORES)
    up_3, down_3, near_2, late_2, swap_1, far_up, far_down = together(
        up_3, down_3, near_2, late_2, swap_1, extra=[((0, 0, cut),), ((1, cut, half - cut),)]
    )

    far_up, far_down = send(far_up, along_z(1)), send(far_down, along_z(-1))
    near_3, late_3 = send(near_2, RING_X), send(late_2, RING_Y)
    swap_2 = send(near_2, CORES)
    late_weights = [[up_2], [down_1], [up_1], [pair]]
    here = (0, 1, 2, 4)
    near_here, late_here = (near_0, near_1, near_2, swap_0), (late_0, late_1, late_2, swap_0)
    subtotal = grad_hidden_part(
        place,
        [
            (here, near_here, (0,) * 4, False, wide, [[down_3], [up_3], [down_2]]),
            (here, late_here, (0, 0, 0, rows), True, 0, late_weights),
        ],
    )
    far_up, far_down, near_3, late_3, swap_2, subtotal = together(
        far_up, far_down, near_3, late_3, swap_2, subtotal
    )

    near_swapped = [swap_0, swap_1, swap_2, send(near_3, CORES)]
    near = ([near_0, near_1, near_2, near_3, *near_swapped], (0,) * 8), False
    late_swapped = [swap_0, swap_1, send(late_2, CORES), send(late_3, CORES)]
    late = ([late_0, late_1, late_2, late_3, *late_swapped], (0,) * 4 + (rows, rows, 0, 0)), True

    make = functools.partial(batch_terms, place, kept_hidden, got_hidden)
    farthest = make(near, wide, 0, 1, cut)
    near_terms = make(near, wide, 1, 3)
    late_first = make(late, wide, 0, 1)
    late_terms = make(late, wide, 1, 3)
    far = [far_up, far_down]
    there = (3, 5, 6, 7)
    near_there, late_there = (near_3, *near_swapped[1:]), (late_3, *late_swapped[1:])
    mine, other = grad_hidden_part(
        place,
        [
            (there, near_there, (0,) * 4, False, 0, [far, [down_3], [up_3], [down_2]]),
            (here, near_here, (0,) * 4, False, 0, [far]),
            (there, late_there, (0, rows, 0, 0), True, 0, late_weights),
        ],
        subtotal,
    )

    upward, downward = send(farthest[0], along_z(1)), send(farthest[1], along_z(-1))
    rise, fall = pass_on(near_terms, 0, near_terms, 1, upward, downward)
    upward, downward = send(rise, along_z(1)), send(fall, along_z(-1))
    upward, downward, other, late_first = together(upward, downward, other, late_first)
    got_other = send(other, PARTNER)
    rise, fall = pass_on(near_terms, 2, late_first, 0, upward, downward)
    upward, downward = send(rise, along_z(1)), send(fall, along_z(-1))
    grads = gate_grads(place, gate_pre.T, up_pre.T, mine, ())
    upward, downward, got_other, *grads = together(upward, downward, got_other, *grads)
    rise, rise_high, fall, fall_high = pass_halves(late_terms, 0, 1, upward, downward, cut)
    kept, got = [], []
    for row, up, down in ((0, rise, fall), (cut, rise_high, fall_high)):
        up, down = send(up, along_z(1)), send(down, along_z(-1))
        own, leaving = last_sum(place, late_terms, 2, row, up, down, kept)
        kept.append(own)
        got.append(send(leaving, PARTNER))
    kept, got = jnp.concatenate(kept, axis=0), jnp.concatenate(got, axis=0)
    grad_down = jnp.concatenate([jnp.where(yh == 0, kept, got), jnp.where(yh == 0, got, kept)], axis=0).T

    grad_gate, grad_up = gate_grads(place, gate_pre.T, up_pre.T, got_other, tuple(grads))
    return grad_gate.T, grad_up.T, grad_down


def solution(mesh):
    inner = Mesh(mesh.devices.reshape(SIZES), AXES)
    dp, tensor = ("yh", "z"), ("x", "yl", "c")
    placed = (P(dp + tensor, None), P(dp, tensor), P(dp, tensor), P(dp, tensor))
    return jax.shard_map(
        local,
        mesh=inner,
        in_specs=placed,
        out_specs=(P(dp, tensor), P(dp, tensor), P(dp, tensor)),
        check_vma=False,
    )
```
